128 devices in a mesh: dp: 8 (over z, x_lo), tensor: 16 (over y, x_hi, core).
Axes of the slice: x: 4 (x_hi: 2, x_lo: 2; x = x_hi * 2 + x_lo), y: 4, z: 4, core: 2. Of those that a mesh axis runs over, the one named last changes fastest.
Arguments:
- tokens: bfloat16 [8, 256, 8192], P('dp', None, 'tensor'), may hold values from -6 to 6
- gain: bfloat16 [8192], replicated, may hold values from 0.3984375 to 1.59375
- q_weight: bfloat16 [8192, 8192], P(None, 'tensor'), may hold values from -1 to 1
- kv_weight: bfloat16 [8192, 2048], P(None, 'tensor'), may hold values from -1 to 1
- o_weight: bfloat16 [8192, 8192], P('tensor'), may hold values from -0.0625 to 0.0625
- out_grad: bfloat16 [8, 256, 8192], P('dp', None, 'tensor'), may hold values from -6 to 6
Outputs:
- output: bfloat16 [8, 256, 8192], P('dp', 'tensor')
- x_grad: bfloat16 [8, 256, 8192], P('dp', 'tensor')
- gain_grad: float32 [8192], P('dp')
- q_grad: float32 [8192, 8192], P('dp', 'tensor')
- kv_grad: float32 [8192, 2048], P('dp', 'tensor')
- o_grad: float32 [8192, 8192], P('tensor', 'dp')
The draws below stay inside these ranges and needn't reach their ends.
All inputs are finite; a program needn't handle non-finite values.
Results may differ from the reference program's by a relative error of at most 0.02.
Values may be sent and summed in bfloat16 or wider, within the bound.
No kernel may reach another device: no remote copies, remote signals or barrier semaphores. Data moves between devices by JAX's collectives and lax.ppermute only.
A program may use at most 192 MiB of HBM per device.

```python
import jax
import jax.numpy as jnp
from jax import lax

D = 8192
HD = 128
QPK = 8
SEQ = 256
KVH = 8
HEADS = 64
GROUPS = 8


def drawn_weight(key, columns):
    return jax.random.truncated_normal(key, -4.0, 4.0, (D, columns), jnp.float32) * D ** (-0.5)


def draw_tokens(key, part):
    key = jax.random.fold_in(key, 7)
    return jax.random.truncated_normal(key, -6.0, 6.0, (GROUPS, SEQ, D), jnp.float32).astype(jnp.bfloat16)


def draw_q_weight(key, part):
    key = jax.random.fold_in(key, 11)
    return drawn_weight(key, HEADS * HD).astype(jnp.bfloat16)


def draw_kv_weight(key, part):
    key = jax.random.fold_in(key, 13)
    return drawn_weight(key, 2 * KVH * HD).astype(jnp.bfloat16)


def levels(own_key, shape, cuts, low, high):
    level = 1.0
    for axis_at, blocks in cuts:
        steps = jax.random.uniform(jax.random.fold_in(jax.random.fold_in(own_key, 6), axis_at), (blocks,), jnp.float32, low / len(cuts), high / len(cuts))
        level = level * jnp.repeat(jnp.exp(steps), shape[axis_at] // blocks).reshape((-1,) + (1,) * (len(shape) - 1 - axis_at))
    return level


def normal_values(rng, shape, spread, limit, cuts=(), held_as=jnp.bfloat16):
    drawn = spread * jax.random.normal(rng, shape, jnp.float32)
    if cuts:
        drawn = drawn * levels(rng, shape, cuts, -0.22, 0.18)
    return jnp.clip(drawn, -limit, limit).astype(held_as)


def setup_inputs(seed: int = 0) -> dict:
    seeds = jax.random.split(jax.random.key(seed), 7)
    return {
        "tokens": draw_tokens(jax.random.fold_in(seeds[6], 71), 0),
        "gain": jnp.clip(1.0 + 0.12 * jax.random.normal(seeds[1], (D,), jnp.float32), 0.3984375, 1.59375).astype(jnp.bfloat16),
        "q_weight": draw_q_weight(jax.random.fold_in(seeds[6], 71), 0),
        "kv_weight": draw_kv_weight(jax.random.fold_in(seeds[6], 71), 0),
        "o_weight": normal_values(seeds[4], (HEADS * HD, D), (HEADS * HD) ** -0.5, 0.0625, ((0, 16),)),
        "out_grad": normal_values(seeds[5], (GROUPS, SEQ, D), 1.0, 6.0, ((0, 8), (2, 16))),
    }


epsilon = 1e-05
theta = 500000.0

def rotary(length, head_size):
    half_dim = head_size // 2
    position = jnp.arange(length, dtype=jnp.float32)
    freq = theta ** (-(jnp.arange(half_dim, dtype=jnp.float32) * 2.0 / head_size))
    angle = position[:, None] * freq[None, :]
    return (jnp.cos(angle), jnp.sin(angle))

def rotate(vectors, cosine_table, sine_table, direction):
    half_dim = vectors.shape[-1] // 2
    first = vectors[..., :half_dim]
    second = vectors[..., half_dim:]
    cos_part = cosine_table[:, None, :]
    sin_part = sine_table[:, None, :] * direction
    return jnp.concatenate([first * cos_part - second * sin_part, second * cos_part + first * sin_part], axis=-1)

def reference(tokens, gain, q_weight, kv_weight, o_weight, out_grad):
    score_scale = HD ** (-0.5)
    cosine_table, sine_table = rotary(SEQ, HD)
    causal = jnp.arange(SEQ)[:, None] >= jnp.arange(SEQ)[None, :]
    gain_float = gain.astype(jnp.float32)
    outputs = []
    grads_in = []
    gain_reduced = jnp.zeros((D,), jnp.float32)
    q_total = jnp.zeros((D, HEADS * HD), jnp.float32)
    kv_total = jnp.zeros((D, 2 * KVH * HD), jnp.float32)
    o_total = jnp.zeros((HEADS * HD, D), jnp.float32)
    for group in range(GROUPS):
        input_tokens = tokens[group].astype(jnp.float32)
        cot_rows = out_grad[group]
        inverse_norm = lax.rsqrt(lax.optimization_barrier(jnp.mean(input_tokens * input_tokens, axis=-1, keepdims=True)) + epsilon)
        standardized_rows = input_tokens * inverse_norm
        normalized_rows = (standardized_rows * gain_float).astype(jnp.bfloat16)
        queries = jnp.dot(normalized_rows, q_weight, preferred_element_type=jnp.float32).reshape(SEQ, HEADS, HD)
        kvproj = jnp.dot(normalized_rows, kv_weight, preferred_element_type=jnp.float32).reshape(SEQ, KVH, 2, HD)
        qrot = rotate(queries, cosine_table, sine_table, 1.0).astype(jnp.bfloat16)
        krot = rotate(kvproj[:, :, 0], cosine_table, sine_table, 1.0).astype(jnp.bfloat16)
        vals = kvproj[:, :, 1].astype(jnp.bfloat16)
        key_full = jnp.repeat(krot, QPK, axis=1).astype(jnp.float32)
        val_full = jnp.repeat(vals, QPK, axis=1).astype(jnp.float32)
        qrot_f = qrot.astype(jnp.float32)
        scores = jnp.einsum('qhd,khd->hqk', qrot_f, key_full) * score_scale
        scores = jnp.where(causal[None], scores, -1e+30)
        probs = jax.nn.softmax(scores, axis=-1)
        pbf = probs.astype(jnp.bfloat16)
        attn = jnp.einsum('hqk,khd->qhd', pbf.astype(jnp.float32), val_full).astype(jnp.bfloat16)
        attn = attn.reshape(SEQ, HEADS * HD)
        mixed = jnp.dot(attn, o_weight, preferred_element_type=jnp.float32)
        outputs.append((input_tokens + mixed).astype(jnp.bfloat16))
        dattn = jnp.dot(cot_rows, o_weight.T, preferred_element_type=jnp.float32).astype(jnp.bfloat16)
        dattn_f = dattn.reshape(SEQ, HEADS, HD).astype(jnp.float32)
        dprobs = jnp.einsum('qhd,khd->hqk', dattn_f, val_full)
        delta = lax.optimization_barrier(jnp.sum(dprobs * probs, axis=-1, keepdims=True))
        dscores = (probs * (dprobs - delta) * score_scale).astype(jnp.bfloat16).astype(jnp.float32)
        dqrot = jnp.einsum('hqk,khd->qhd', dscores, key_full)
        dkrot = jnp.einsum('hqk,qhd->khd', dscores, qrot_f).reshape(SEQ, KVH, QPK, HD).sum(axis=2)
        dvals = jnp.einsum('hqk,qhd->khd', pbf.astype(jnp.float32), dattn_f).reshape(SEQ, KVH, QPK, HD).sum(axis=2)
        dq = rotate(dqrot, cosine_table, sine_table, -1.0).astype(jnp.bfloat16).reshape(SEQ, HEADS * HD)
        dk = rotate(dkrot, cosine_table, sine_table, -1.0).astype(jnp.bfloat16)
        dkv = jnp.stack([dk, dvals.astype(jnp.bfloat16)], axis=2).reshape(SEQ, 2 * KVH * HD)
        normalized_gradient = jnp.dot(dq, q_weight.T, preferred_element_type=jnp.float32) + jnp.dot(dkv, kv_weight.T, preferred_element_type=jnp.float32)
        scaled_gradient = normalized_gradient * gain_float
        input_gradient = inverse_norm * (scaled_gradient - standardized_rows * lax.optimization_barrier(jnp.mean(scaled_gradient * standardized_rows, axis=-1, keepdims=True)))
        grads_in.append((cot_rows.astype(jnp.float32) + input_gradient).astype(jnp.bfloat16))
        gain_reduced = gain_reduced + lax.optimization_barrier(jnp.sum(normalized_gradient * standardized_rows, axis=0))
        q_term = lax.optimization_barrier(jnp.dot(normalized_rows.T, dq, preferred_element_type=jnp.float32).astype(jnp.bfloat16))
        kv_term = lax.optimization_barrier(jnp.dot(normalized_rows.T, dkv, preferred_element_type=jnp.float32).astype(jnp.bfloat16))
        o_term = lax.optimization_barrier(jnp.dot(attn.T, cot_rows, preferred_element_type=jnp.float32).astype(jnp.bfloat16))
        q_total = q_total + q_term.astype(jnp.float32)
        kv_total = kv_total + kv_term.astype(jnp.float32)
        o_total = o_total + o_term.astype(jnp.float32)
    return (jnp.stack(outputs), jnp.stack(grads_in), gain_reduced, q_total, kv_total, o_total)
```

```python
import jax
import jax.numpy as jnp
from jax import lax
from jax.experimental import pallas as pl
from jax.experimental.pallas import tpu as pltpu
from jax.sharding import PartitionSpec as P

epsilon = 1e-05
theta = 500000.0
f32 = jnp.float32
bf16 = jnp.bfloat16
VMEM = 48 * 1024 * 1024


def partner(array, axis, bits):
    return lax.ppermute(array, axis, [(i, i ^ bits) for i in range(lax.axis_size(axis))])


def rotary(length, head_size):
    half_dim = head_size // 2
    position = jnp.arange(length, dtype=f32)
    freq = theta ** (-(jnp.arange(half_dim, dtype=f32) * 2.0 / head_size))
    angle = position[:, None] * freq[None, :]
    return (jnp.cos(angle), jnp.sin(angle))


def rotate(vectors, cosine_table, sine_table, direction):
    half_dim = vectors.shape[-1] // 2
    first = vectors[..., :half_dim]
    second = vectors[..., half_dim:]
    cos_part = cosine_table[:, None, :]
    sin_part = sine_table[:, None, :] * direction
    return jnp.concatenate(
        [first * cos_part - second * sin_part, second * cos_part + first * sin_part], axis=-1
    )


def contract_rows(left, right):
    return lax.dot_general(left, right, (((0,), (0,)), ((), ())), preferred_element_type=f32)


def gather_blocks(shard):
    blocks = {0: shard, 2: partner(shard, "tensor", 2)}
    for k in (4, 12, 8):
        blocks[k] = partner(shard, "tensor", k)
    for k in (4, 12, 8):
        blocks[k ^ 2] = partner(blocks[2], "tensor", k)
    for k in range(0, 16, 2):
        blocks[k ^ 1] = partner(blocks[k], "tensor", 1)
    return [blocks[k] for k in range(16)]


def norm_kernel(at_ref, gain_ref, *refs):
    blocks, (normed_ref, inverse_ref, own_ref) = refs[:16], refs[16:]
    me = at_ref[0]
    rows = inverse_ref.shape[0]
    width = blocks[0].shape[1]

    @pl.loop(0, rows // 16)
    def _(step):
        here = pl.ds(pl.multiple_of(step * 16, 16), 16)
        squares = jnp.zeros((16, width), f32)
        for block in blocks:
            value = block[here, :].astype(f32)
            squares += value * value
        mean = jnp.sum(squares, axis=-1, keepdims=True) / (16 * width)
        inverse = lax.rsqrt(mean + epsilon)
        inverse_ref[here, :] = inverse
        for k, block in enumerate(blocks):
            columns = pl.ds(pl.multiple_of((me ^ k) * width, width), width)
            value = block[here, :].astype(f32)
            normed_ref[here, columns] = (value * inverse * gain_ref[:, columns]).astype(bf16)

        @pl.when(pl.program_id(0) * (rows // 16) + step == me)
        def _():
            for k, block in enumerate(blocks):
                columns = pl.ds(pl.multiple_of((me ^ k) * width, width), width)
                own_ref[:, columns] = block[here, :]


def join_kernel(at_ref, *refs):
    blocks, out_ref = refs[:16], refs[16]
    me = at_ref[0]
    width = blocks[0].shape[1]
    for k, block in enumerate(blocks):
        columns = pl.ds(pl.multiple_of((me ^ k) * width, width), width)
        out_ref[:, columns] = block[...]


def join(me, blocks, tile=64):
    length, width = blocks[0].shape
    return pl.pallas_call(
        join_kernel,
        grid_spec=pltpu.PrefetchScalarGridSpec(
            num_scalar_prefetch=1,
            grid=(length // tile,),
            in_specs=[pl.BlockSpec((tile, width), lambda i, at: (i, 0))] * 16,
            out_specs=pl.BlockSpec((tile, 16 * width), lambda i, at: (i, 0)),
        ),
        out_shape=jax.ShapeDtypeStruct((length, 16 * width), bf16),
        compiler_params=pltpu.CompilerParams(vmem_limit_bytes=VMEM),
        name="join",
    )(me, *blocks)


def norm(me, gain_row, blocks, tile=64):
    length, width = blocks[0].shape
    whole = 16 * width
    return pl.pallas_call(
        norm_kernel,
        grid_spec=pltpu.PrefetchScalarGridSpec(
            num_scalar_prefetch=1,
            grid=(length // tile,),
            in_specs=[pl.BlockSpec((1, whole), lambda i, at: (0, 0))]
            + [pl.BlockSpec((tile, width), lambda i, at: (i, 0))] * 16,
            out_specs=[
                pl.BlockSpec((tile, whole), lambda i, at: (i, 0)),
                pl.BlockSpec((tile, 1), lambda i, at: (i, 0)),
                pl.BlockSpec((16, whole), lambda i, at: (0, 0)),
            ],
        ),
        out_shape=[
            jax.ShapeDtypeStruct((length, whole), bf16),
            jax.ShapeDtypeStruct((length, 1), f32),
            jax.ShapeDtypeStruct((16, whole), bf16),
        ],
        compiler_params=pltpu.CompilerParams(vmem_limit_bytes=VMEM),
        name="norm",
    )(me, gain_row, *blocks)


def scatter_rows(partial, core, y_at, x_at):
    rows = partial.reshape(4, 2, 2, 16, partial.shape[1])
    core_rows = lax.dynamic_index_in_dim(rows, core, 2, keepdims=False)
    other_rows = lax.dynamic_index_in_dim(rows, 1 - core, 2, keepdims=False)
    arrived = partner(other_rows.astype(bf16), "tensor", 1)
    summed = (core_rows.astype(f32) + arrived.astype(f32)).astype(bf16)
    total = lax.dynamic_index_in_dim(summed, y_at, 0, keepdims=False).astype(f32)
    for k in (1, 3, 2):
        message = lax.dynamic_index_in_dim(summed, y_at ^ k, 0, keepdims=False)
        total += partner(message, "tensor", 4 * k).astype(f32)
    kept = lax.dynamic_index_in_dim(total, x_at, 0, keepdims=False)
    message = lax.dynamic_index_in_dim(total, 1 - x_at, 0, keepdims=False).astype(bf16)
    return kept + partner(message, "tensor", 2).astype(f32)


def exchange_columns(whole, dp_at, core, width):
    blocks = []
    for k in range(8):
        at = (2 * (dp_at ^ k) + core) * width
        message = lax.dynamic_slice_in_dim(whole, at, width, 1)
        blocks.append(partner(message, "dp", k) if k else message)
    return jnp.concatenate(blocks, 0)


def gather_dp(shard):
    blocks = {0: shard, 1: partner(shard, "dp", 1)}
    for k in (2, 6, 4):
        blocks[k] = partner(shard, "dp", k)
        blocks[k ^ 1] = partner(blocks[1], "dp", k)
    return jnp.concatenate([blocks[k] for k in range(8)], 0)


def on_device(tokens, gain, q_weight, kv_weight, o_weight, out_grad):
    t_at = lax.axis_index("tensor")
    dp_at = lax.axis_index("dp")
    core, x_at, y_at = t_at % 2, t_at // 2 % 2, t_at // 4
    me = t_at[None].astype(jnp.int32)
    is_even = core == 0
    length, width = tokens.shape[1:]
    head_size = kv_weight.shape[1]
    local_heads = q_weight.shape[1] // head_size
    score_scale = head_size ** (-0.5)
    cosine_table, sine_table = rotary(length, head_size)
    causal = jnp.arange(length)[:, None] >= jnp.arange(length)[None, :]
    gain_float = gain.astype(f32)

    normed, inverse_norm, own_tokens = norm(me, gain_float[None, :], gather_blocks(tokens[0]))
    cotangent = join(me, gather_blocks(out_grad[0]))

    normed_columns = exchange_columns(normed, dp_at, core, width)
    cot_columns = exchange_columns(cotangent, dp_at, core, width)
    normed_other = partner(normed_columns, "tensor", 1)
    cot_other = partner(cot_columns, "tensor", 1)

    kv_own = jnp.dot(normed, kv_weight, preferred_element_type=f32)
    kv_rot = rotate(kv_own[:, None, :], cosine_table, sine_table, 1.0)[:, 0]
    kv_own = jnp.where(is_even, kv_rot, kv_own).astype(bf16)
    kv_other = partner(kv_own, "tensor", 1)
    key_rows = jnp.where(is_even, kv_own, kv_other)
    value_rows = jnp.where(is_even, kv_other, kv_own)
    queries = jnp.dot(normed, q_weight, preferred_element_type=f32).reshape(
        length, local_heads, head_size
    )
    qrot = rotate(queries, cosine_table, sine_table, 1.0).astype(bf16)
    scores = jnp.einsum("qhd,kd->hqk", qrot, key_rows, preferred_element_type=f32) * score_scale
    scores = jnp.where(causal[None], scores, -1e30)
    top_score = jnp.max(scores, axis=-1, keepdims=True)
    expo = jnp.exp(scores - top_score)
    probs = expo / jnp.sum(expo, axis=-1, keepdims=True)
    pbf = probs.astype(bf16)
    attn = jnp.einsum("hqk,kd->qhd", pbf, value_rows, preferred_element_type=f32).astype(bf16)
    attn = attn.reshape(length, local_heads * head_size)
    attn_all = gather_dp(attn)

    mixed = scatter_rows(jnp.dot(attn, o_weight, preferred_element_type=f32), core, y_at, x_at)
    result = (own_tokens.astype(f32) + mixed).astype(bf16)

    dattn = jnp.dot(cotangent, o_weight.T, preferred_element_type=f32).astype(bf16)
    dattn = dattn.reshape(length, local_heads, head_size)
    dprobs = jnp.einsum("qhd,kd->hqk", dattn, value_rows, preferred_element_type=f32)
    delta = jnp.sum(dprobs * probs, axis=-1, keepdims=True)
    dscores = (probs * (dprobs - delta) * score_scale).astype(bf16)
    dqrot = jnp.einsum("hqk,kd->qhd", dscores, key_rows, preferred_element_type=f32)
    dkey_part = jnp.einsum("hqk,qhd->kd", dscores, qrot, preferred_element_type=f32)
    dvalue_part = jnp.einsum("hqk,qhd->kd", pbf, dattn, preferred_element_type=f32)
    outgoing = jnp.where(is_even, dvalue_part, dkey_part)
    incoming = partner(outgoing.astype(bf16), "tensor", 1).astype(f32)
    own_total = jnp.where(is_even, dkey_part, dvalue_part) + incoming
    unrotated = rotate(own_total[:, None, :], cosine_table, sine_table, -1.0)[:, 0]
    own_grad = jnp.where(is_even, unrotated, own_total).astype(bf16)
    dq_rows = (
        rotate(dqrot, cosine_table, sine_table, -1.0)
        .astype(bf16)
        .reshape(length, local_heads * head_size)
    )
    d_all = gather_dp(jnp.concatenate([dq_rows, own_grad], axis=1))

    q_part = jnp.dot(dq_rows, q_weight.T, preferred_element_type=f32)
    kv_part = jnp.dot(own_grad, kv_weight.T, preferred_element_type=f32)
    normed_gradient_part = q_part + kv_part
    gain_part = jnp.sum(normed_gradient_part * normed.astype(f32), axis=0) / gain_float
    normalized_gradient = scatter_rows(normed_gradient_part, core, y_at, x_at)

    gain_part = gain_part.reshape(8, -1)
    gain_grad = lax.dynamic_index_in_dim(gain_part, dp_at, 0, keepdims=False)
    for k in range(1, 8):
        gain_grad += partner(
            lax.dynamic_index_in_dim(gain_part, dp_at ^ k, 0, keepdims=False), "dp", k
        )
    for k in (1, 2, 4, 8):
        gain_grad += partner(gain_grad, "tensor", k)

    own_inverse = lax.dynamic_slice_in_dim(inverse_norm, t_at * 16, 16, 0)
    own_cot = lax.dynamic_slice_in_dim(cotangent, t_at * 16, 16, 0)
    local_standardized = own_tokens.astype(f32) * own_inverse
    scaled_gradient = normalized_gradient * gain_float
    input_gradient = own_inverse * (
        scaled_gradient
        - local_standardized
        * jnp.mean(scaled_gradient * local_standardized, axis=-1, keepdims=True)
    )
    input_grad = (own_cot.astype(f32) + input_gradient).astype(bf16)

    def ordered(own, other, axis):
        return jnp.where(
            is_even,
            jnp.concatenate([own, other], axis),
            jnp.concatenate([other, own], axis),
        )

    o_grad = ordered(contract_rows(attn_all, cot_columns), contract_rows(attn_all, cot_other), 1)
    qkv_grad = ordered(contract_rows(normed_columns, d_all), contract_rows(normed_other, d_all), 0)
    q_width = q_weight.shape[1]
    return (
        result[None],
        input_grad[None],
        gain_grad,
        qkv_grad[:, :q_width],
        qkv_grad[:, q_width:],
        o_grad,
    )


def solution(mesh):
    in_specs = (
        P("dp", None, "tensor"),
        P(),
        P(None, "tensor"),
        P(None, "tensor"),
        P("tensor", None),
        P("dp", None, "tensor"),
    )
    out_specs = (
        P("dp", "tensor", None),
        P("dp", "tensor", None),
        P("dp"),
        P("dp", "tensor"),
        P("dp", "tensor"),
        P("tensor", "dp"),
    )
    return jax.shard_map(
        on_device, mesh=mesh, in_specs=in_specs, out_specs=out_specs, check_vma=False
    )
```

```python
import jax
import jax.numpy as jnp
import numpy as np
from jax import lax
from jax.experimental import pallas as pl
from jax.experimental.pallas import tpu as pltpu
from jax.sharding import PartitionSpec as P

epsilon = 1e-05
theta = 500000.0
f32 = jnp.float32
bf16 = jnp.bfloat16
VMEM = 20 * 1024 * 1024
ANY = pl.BlockSpec(memory_space=pl.ANY)
T, CHIP, CORE, Y, X, Z, XL = range(7)


def partner(array, axis, bits):
    return lax.ppermute(array, axis, [(i, i ^ bits) for i in range(lax.axis_size(axis))])


class Order:
    def __init__(self, at):
        self.at, self.last = at, []

    def wait(self, *arrays):
        self.last = self.last + list(arrays)


def call(kernel, name, order, operands, outputs, grid=(1,), scratch=()):
    arrays = [array for array, _ in operands]
    after = [a for a in order.last if not any(a is b for b in arrays)]
    count, extra = len(arrays), len(after)

    def body(at_ref, *refs):
        kernel(at_ref, *refs[:count], *refs[count + extra :])

    results = pl.pallas_call(
        body,
        grid_spec=pltpu.PrefetchScalarGridSpec(
            num_scalar_prefetch=1,
            grid=grid,
            in_specs=[spec for _, spec in operands] + [ANY] * extra,
            out_specs=[spec for _, spec in outputs],
            scratch_shapes=list(scratch),
        ),
        out_shape=[shape for shape, _ in outputs],
        compiler_params=pltpu.CompilerParams(vmem_limit_bytes=VMEM),
        cost_estimate=pl.CostEstimate(flops=1, bytes_accessed=1, transcendentals=0),
        name=name,
    )(order.at, *arrays, *after)
    order.last = [results[0]]
    return results


def whole(array):
    rank = len(array.shape)
    return (array, pl.BlockSpec(tuple(array.shape), lambda *_: (0,) * rank))


def shape(dims, dtype=bf16):
    return jax.ShapeDtypeStruct(tuple(dims), dtype)


def nt(left, right):
    return lax.dot_general(left, right, (((1,), (1,)), ((), ())), preferred_element_type=f32)


def tn(left, right):
    return lax.dot_general(left, right, (((0,), (0,)), ((), ())), preferred_element_type=f32)


def nn(left, right):
    return jnp.dot(left, right, preferred_element_type=f32)


def move(name, order, sources, out_shapes, plan):
    count, outs_count = len(sources), len(out_shapes)

    def kernel(at_ref, *refs):
        ins, outs = refs[:count], refs[count : count + outs_count]
        held, sems, out_sems = refs[count + outs_count : -2], refs[-2], refs[-1]
        copies = [
            pltpu.make_async_copy(source, target, sems.at[number])
            for number, (source, target) in enumerate(plan(at_ref, ins, held))
        ]
        for copy in copies:
            copy.start()
        for copy in copies:
            copy.wait()
        copies = [
            pltpu.make_async_copy(source, target, out_sems.at[number])
            for number, (source, target) in enumerate(zip(held, outs))
        ]
        for copy in copies:
            copy.start()
        for copy in copies:
            copy.wait()

    return call(
        kernel,
        name,
        order,
        [(source, ANY) for source in sources],
        [(s, ANY) for s in out_shapes],
        scratch=[pltpu.VMEM(s.shape, s.dtype) for s in out_shapes]
        + [pltpu.SemaphoreType.DMA((16,))] * 2,
    )


def stack(name, order, *groups):
    groups = [[p if p.ndim == 3 else p[None] for p in group] for group in groups]
    sources = [p for group in groups for p in group]

    def plan(at_ref, ins, outs):
        pairs, number = [], 0
        for group, out in zip(groups, outs):
            row = 0
            for p in group:
                pairs.append((ins[number], out.at[pl.ds(row, p.shape[0])]))
                row += p.shape[0]
                number += 1
        return pairs

    outs = [shape((sum(p.shape[0] for p in g),) + g[0].shape[1:]) for g in groups]
    return move(name, order, sources, outs, plan)


def norm(order, gain_row, own, other):
    chips, length, width = own.shape
    tile = 64
    full = 2 * chips * width

    def kernel(at_ref, gain_ref, own_ref, other_ref, normed_ref, inverse_ref, rows_ref):
        chip, core = at_ref[CHIP], at_ref[CORE]

        def columns(pair, half):
            return pl.ds(pl.multiple_of((2 * pair + half) * width, width), width)

        @pl.loop(0, tile // 16)
        def _(step):
            here = pl.ds(pl.multiple_of(step * 16, 16), 16)
            squares = jnp.zeros((16, width), f32)
            for j in range(chips):
                for ref in (own_ref, other_ref):
                    value = ref[j, here, :].astype(f32)
                    squares += value * value
            mean = jnp.sum(squares, axis=-1, keepdims=True) / full
            inverse = lax.rsqrt(mean + epsilon)
            inverse_ref[here, :] = inverse
            for j in range(chips):
                for ref, half in ((own_ref, core), (other_ref, 1 - core)):
                    place = columns(chip ^ j, half)
                    value = ref[j, here, :].astype(f32)
                    normed_ref[here, place] = (value * inverse * gain_ref[:, place]).astype(bf16)

            @pl.when(pl.program_id(0) * (tile // 16) + step == at_ref[T])
            def _():
                for j in range(chips):
                    for ref, half in ((own_ref, core), (other_ref, 1 - core)):
                        rows_ref[:, columns(chip ^ j, half)] = ref[j, here, :]

    block = pl.BlockSpec((chips, tile, width), lambda i, at: (0, i, 0))
    return call(
        kernel,
        "norm",
        order,
        [whole(gain_row), (own, block), (other, block)],
        [
            (shape((length, full)), pl.BlockSpec((tile, full), lambda i, at: (i, 0))),
            (shape((length, 1), f32), pl.BlockSpec((tile, 1), lambda i, at: (i, 0))),
            (shape((16, full)), pl.BlockSpec((16, full), lambda i, at: (0, 0))),
        ],
        grid=(length // tile,),
    )


def pick_tokens(order, own):
    chips, length, width = own.shape

    def kernel(at_ref, own_ref, *out):
        for k in range(4):
            for x in range(2):
                block = own_ref[at_ref[CHIP] ^ (2 * (at_ref[Z] ^ k) + x)]
                out[k][x] = block.T

    return call(
        kernel, "pick_tokens", order, [whole(own)], [whole_out((2, width, length))] * 4
    )


def turned(value, cos_ref, sin_ref, direction):
    swapped = pltpu.roll(value, value.shape[-1] // 2, 1)
    return value * cos_ref[...] + swapped * (sin_ref[...] * direction)


def project(order, normed, q_weight, kv_weight, tables):
    length, full = normed.shape
    q_width, head = q_weight.shape[1], kv_weight.shape[1]
    tile = 1024

    def kernel(at_ref, x_ref, q_ref, kv_ref, cos_ref, sin_ref, rot_ref, own_ref, qacc, kvacc):
        step = pl.program_id(0)

        @pl.when(step == 0)
        def _():
            qacc[...] = jnp.zeros_like(qacc)
            kvacc[...] = jnp.zeros_like(kvacc)

        qacc[...] += nn(x_ref[...], q_ref[...])
        kvacc[...] += nn(x_ref[...], kv_ref[...])

        @pl.when(step == pl.num_programs(0) - 1)
        def _():
            for h in range(q_width // head):
                place = slice(h * head, (h + 1) * head)
                rot_ref[:, place] = turned(qacc[:, place], cos_ref, sin_ref, 1.0).astype(bf16)
            plain = kvacc[...]
            rotated = turned(plain, cos_ref, sin_ref, 1.0)
            own_ref[...] = jnp.where(at_ref[CORE] == 0, rotated, plain).astype(bf16)

    return call(
        kernel,
        "project",
        order,
        [
            (normed, pl.BlockSpec((length, tile), lambda i, at: (0, i))),
            (q_weight, pl.BlockSpec((tile, q_width), lambda i, at: (i, 0))),
            (kv_weight, pl.BlockSpec((tile, head), lambda i, at: (i, 0))),
            whole(tables[0]),
            whole(tables[1]),
        ],
        [whole_out((length, q_width)), whole_out((length, head))],
        grid=(full // tile,),
        scratch=[pltpu.VMEM((length, q_width), f32), pltpu.VMEM((length, head), f32)],
    )


def whole_out(dims, dtype=bf16):
    return whole(shape(dims, dtype))


def attend(order, rot, own, other):
    length, q_width = rot.shape
    head = own.shape[1]
    heads = q_width // head
    scale = head ** (-0.5)

    def kernel(at_ref, rot_ref, own_ref, other_ref, attn_ref, probs_ref, turned_ref):
        even = at_ref[CORE] == 0
        key = jnp.where(even, own_ref[...], other_ref[...])
        value = jnp.where(even, other_ref[...], own_ref[...])
        row = lax.broadcasted_iota(jnp.int32, (length, length), 0)
        column = lax.broadcasted_iota(jnp.int32, (length, length), 1)
        for h in range(heads):
            place = slice(h * head, (h + 1) * head)
            scores = jnp.where(row >= column, nt(rot_ref[:, place], key) * scale, -1e30)
            expo = jnp.exp(scores - jnp.max(scores, axis=-1, keepdims=True))
            probs = expo / jnp.sum(expo, axis=-1, keepdims=True)
            probs_ref[h] = probs
            attn = nn(probs.astype(bf16), value)
            attn_ref[:, place] = attn.astype(bf16)
            turned_ref[place, :] = attn.T.astype(bf16)

    return call(
        kernel,
        "attend",
        order,
        [whole(rot), whole(own), whole(other)],
        [
            whole_out((length, q_width)),
            whole_out((heads, length, length), f32),
            whole_out((q_width, length)),
        ],
    )


def split_rows(at_ref, product, rows_ref, send_ref, keep_ref):
    rows_ref[...] = product.reshape(rows_ref.shape)
    send_ref[...] = rows_ref[:, 1 - at_ref[CORE]].astype(bf16)
    keep_ref[...] = rows_ref[:, at_ref[CORE]].astype(bf16)


def mix(order, attn, o_weight):
    length, q_width = attn.shape
    full = o_weight.shape[1]
    tile = 1024

    def kernel(at_ref, attn_ref, w_ref, send_ref, keep_ref, rows_ref):
        split_rows(at_ref, nn(attn_ref[...], w_ref[...]), rows_ref, send_ref, keep_ref)

    out = (shape((length // 32, 16, full)), pl.BlockSpec((length // 32, 16, tile), lambda i, at: (0, 0, i)))
    return call(
        kernel,
        "mix",
        order,
        [whole(attn), (o_weight, pl.BlockSpec((q_width, tile), lambda i, at: (0, i)))],
        [out, out],
        grid=(full // tile,),
        scratch=[pltpu.VMEM((length // 32, 2, 16, tile), f32)],
    )


def pair_sum(order, keep, arrived, groups, index):
    chips, _, full = keep.shape
    each = chips // groups
    tile = 2048

    def kernel(at_ref, keep_ref, arrived_ref, *out):
        for k in range(groups):
            here = pl.ds((at_ref[index] ^ k) * each, each) if groups > 1 else slice(None)
            out[k][...] = (keep_ref[here].astype(f32) + arrived_ref[here].astype(f32)).astype(bf16)

    block = pl.BlockSpec((chips, 16, tile), lambda i, at: (0, 0, i))
    out = (shape((each, 16, full)), pl.BlockSpec((each, 16, tile), lambda i, at: (0, 0, i)))
    return call(
        kernel,
        "pair_sum",
        order,
        [(keep, block), (arrived, block)],
        [out] * groups,
        grid=(full // tile,),
    )


def ring_sum(order, parts):
    _, _, full = parts[0].shape
    tile = 2048

    def kernel(at_ref, *refs):
        parts, keep_ref, send_ref = refs[:4], refs[4], refs[5]
        for target, x in ((keep_ref, at_ref[X]), (send_ref, 1 - at_ref[X])):
            total = parts[0][x].astype(f32)
            for part in parts[1:]:
                total += part[x].astype(f32)
            target[...] = total.astype(target.dtype)

    block = pl.BlockSpec((2, 16, tile), lambda i, at: (0, 0, i))
    out = pl.BlockSpec((16, tile), lambda i, at: (0, i))
    return call(
        kernel,
        "ring_sum",
        order,
        [(part, block) for part in parts],
        [(shape((16, full), f32), out), (shape((16, full)), out)],
        grid=(full // tile,),
    )


def out_gradient(order, own, other, o_weight):
    chips, length, width = own.shape
    q_width, full = o_weight.shape

    def kernel(at_ref, own_ref, other_ref, w_ref, dattn_ref, rows_ref, acc):
        step = pl.program_id(0)
        core = at_ref[CORE]

        @pl.when(step == 0)
        def _():
            acc[...] = jnp.zeros_like(acc)

        mine = pl.ds(pl.multiple_of(at_ref[T] * 16, 16), 16)
        for ref, half in ((own_ref, core), (other_ref, 1 - core)):
            place = pl.ds(pl.multiple_of(half * width, width), width)
            acc[...] += nt(ref[0], w_ref[:, place])
            rows_ref[:, place] = ref[0, mine, :]

        @pl.when(step == pl.num_programs(0) - 1)
        def _():
            dattn_ref[...] = acc[...].astype(bf16)

    block = pl.BlockSpec((1, length, width), lambda i, at: (i, 0, 0))
    return call(
        kernel,
        "out_gradient",
        order,
        [
            (own, block),
            (other, block),
            (o_weight, pl.BlockSpec((q_width, 2 * width), lambda i, at: (0, at[CHIP] ^ i))),
        ],
        [
            whole_out((length, q_width)),
            (shape((16, full)), pl.BlockSpec((16, 2 * width), lambda i, at: (0, at[CHIP] ^ i))),
        ],
        grid=(chips,),
        scratch=[pltpu.VMEM((length, q_width), f32)],
    )


def attend_gradient(order, dattn, probs, rot, own, other, tables):
    length, q_width = rot.shape
    head = own.shape[1]
    scale = head ** (-0.5)

    def kernel(
        at_ref, dattn_ref, probs_ref, rot_ref, own_ref, other_ref, cos_ref, sin_ref,
        dq_ref, keep_ref, send_ref,
    ):
        even = at_ref[CORE] == 0
        key = jnp.where(even, own_ref[...], other_ref[...])
        value = jnp.where(even, other_ref[...], own_ref[...])
        dkey = jnp.zeros((length, head), f32)
        dvalue = jnp.zeros((length, head), f32)
        for h in range(q_width // head):
            place = slice(h * head, (h + 1) * head)
            probs = probs_ref[h]
            dattn = dattn_ref[:, place]
            dprobs = nt(dattn, value)
            delta = jnp.sum(dprobs * probs, axis=-1, keepdims=True)
            dscores = (probs * (dprobs - delta) * scale).astype(bf16)
            dq_ref[:, place] = turned(nn(dscores, key), cos_ref, sin_ref, -1.0).astype(bf16)
            dkey += tn(dscores, rot_ref[:, place])
            dvalue += tn(probs.astype(bf16), dattn)
        keep_ref[...] = jnp.where(even, dkey, dvalue)
        send_ref[...] = jnp.where(even, dvalue, dkey).astype(bf16)

    return call(
        kernel,
        "attend_gradient",
        order,
        [whole(a) for a in (dattn, probs, rot, own, other, *tables)],
        [whole_out((length, q_width)), whole_out((length, head), f32), whole_out((length, head))],
    )


def join_gradient(order, dq, keep, arrived, inverse, tables):
    length, q_width = dq.shape
    head = keep.shape[1]

    def kernel(
        at_ref, dq_ref, keep_ref, arrived_ref, inverse_ref, cos_ref, sin_ref, out_ref, scaled_ref
    ):
        inverse = inverse_ref[...]
        dq = dq_ref[...]
        out_ref[:, :q_width] = dq
        scaled_ref[:, :q_width] = (dq.astype(f32) * inverse).astype(bf16)
        plain = keep_ref[...] + arrived_ref[...].astype(f32)
        back = turned(plain, cos_ref, sin_ref, -1.0)
        own = jnp.where(at_ref[CORE] == 0, back, plain).astype(bf16)
        out_ref[:, q_width:] = own
        scaled_ref[:, q_width:] = (own.astype(f32) * inverse).astype(bf16)

    return call(
        kernel,
        "join_gradient",
        order,
        [whole(a) for a in (dq, keep, arrived, inverse, *tables)],
        [whole_out((length, q_width + head))] * 2,
    )


def norm_gradient(order, dqkv, q_weight, kv_weight, normed, gain_row):
    length, full = normed.shape
    q_width, head = q_weight.shape[1], kv_weight.shape[1]
    tile = 1024

    def kernel(
        at_ref, d_ref, q_ref, kv_ref, normed_ref, gain_ref, send_ref, keep_ref, part_ref, rows_ref
    ):
        product = nt(d_ref[:, :q_width], q_ref[...]) + nt(d_ref[:, q_width:], kv_ref[...])
        part = jnp.sum(product * normed_ref[...].astype(f32), axis=0, keepdims=True)
        part_ref[0] = part / gain_ref[...]
        split_rows(at_ref, product, rows_ref, send_ref, keep_ref)

    out = (shape((length // 32, 16, full)), pl.BlockSpec((length // 32, 16, tile), lambda i, at: (0, 0, i)))
    return call(
        kernel,
        "norm_gradient",
        order,
        [
            whole(dqkv),
            (q_weight, pl.BlockSpec((tile, q_width), lambda i, at: (i, 0))),
            (kv_weight, pl.BlockSpec((tile, head), lambda i, at: (i, 0))),
            (normed, pl.BlockSpec((length, tile), lambda i, at: (0, i))),
            (gain_row, pl.BlockSpec((1, tile), lambda i, at: (0, i))),
        ],
        [out, out, (shape((full // tile, 1, tile), f32), pl.BlockSpec((1, 1, tile), lambda i, at: (i, 0, 0)))],
        grid=(full // tile,),
        scratch=[pltpu.VMEM((length // 32, 2, 16, tile), f32)],
    )


def input_gradient(order, keep, arrived, tokens, inverse, cotangent, gain_row):
    rows, full = tokens.shape

    def kernel(
        at_ref, keep_ref, arrived_ref, tokens_ref, inverse_ref, cot_ref, gain_ref, out_ref,
        xhat_ref, scaled_ref,
    ):
        inverse = inverse_ref[pl.ds(pl.multiple_of(at_ref[T] * 16, 16), 16), :]
        tile = 1024
        dots = jnp.zeros((rows, tile), f32)
        for i in range(full // tile):
            place = slice(i * tile, (i + 1) * tile)
            total = keep_ref[:, place] + arrived_ref[:, place].astype(f32)
            xhat = tokens_ref[:, place].astype(f32) * inverse
            scaled = total * gain_ref[:, place]
            xhat_ref[:, place] = xhat
            scaled_ref[:, place] = scaled
            dots += scaled * xhat
        mean = jnp.sum(dots, axis=-1, keepdims=True) / full
        for i in range(full // tile):
            place = slice(i * tile, (i + 1) * tile)
            change = inverse * (scaled_ref[:, place] - xhat_ref[:, place] * mean)
            out_ref[:, place] = (cot_ref[:, place].astype(f32) + change).astype(bf16)

    return call(
        kernel,
        "input_gradient",
        order,
        [whole(a) for a in (keep, arrived, tokens, inverse, cotangent, gain_row)],
        [whole_out((rows, full))],
        scratch=[pltpu.VMEM((rows, full), f32)] * 2,
    )[0]


def out_terms(order, own, other, rows):
    _, length, width = own.shape
    total = rows[0].shape[0]

    def kernel(at_ref, own_ref, other_ref, *refs):
        rows, (send_ref, keep_ref, acc) = refs[:4], refs[4:]
        step = pl.program_id(0)

        def add(ref):
            acc[...] = nn(rows[0][...], ref[0, 0])
            for k in range(1, 4):
                acc[...] += nn(rows[k][...], ref[k, 0])

        pl.when(step % 2 == 0)(lambda: add(own_ref))
        pl.when(step % 2 == 1)(lambda: add(other_ref))

        @pl.when(step < 2)
        def _():
            send_ref[...] = acc[...].astype(bf16)

        @pl.when(step >= 2)
        def _():
            keep_ref[...] = acc[...]

    def x_of(i, at):
        return jnp.where(i < 2, 1 - at[XL], at[XL])

    def side(half, at):
        return jnp.where(half == 0, at[CORE], 1 - at[CORE])

    block = pl.BlockSpec((4, 1, length, width), lambda i, at: (0, x_of(i, at), 0, 0))
    dims = (4, 2, length, width)
    return call(
        kernel,
        "out_terms",
        order,
        [(own.reshape(dims), block), (other.reshape(dims), block)] + [whole(a) for a in rows],
        [
            (
                shape((total, 2 * width)),
                pl.BlockSpec((total, width), lambda i, at: (0, side(jnp.minimum(i, 1), at))),
            ),
            (
                shape((total, 2 * width), f32),
                pl.BlockSpec((total, width), lambda i, at: (0, side(jnp.maximum(i - 2, 0), at))),
            ),
        ],
        grid=(4,),
        scratch=[pltpu.VMEM((total, width), f32)],
    )


def q_gradient(order, own, other, rows, gain_column, q_width):
    _, width, length = own[0].shape
    total = rows[0].shape[2]

    def kernel(at_ref, *refs):
        blocks, row_refs, gain_ref, q_ref, kv_ref, acc = refs[:4], refs[4:8], *refs[8:]
        half, k = pl.program_id(0), pl.program_id(1)

        def add(pair):
            for number in range(4):

                @pl.when(k == number)
                def _():
                    term = nn(pair[0][0], row_refs[number][0]) + nn(pair[1][0], row_refs[number][1])
                    if number == 0:
                        acc[...] = term
                    else:
                        acc[...] += term

        pl.when(half == 0)(lambda: add(blocks[:2]))
        pl.when(half == 1)(lambda: add(blocks[2:]))

        @pl.when(k == 3)
        def _():
            product = acc[...] * gain_ref[...]
            q_ref[...] = product[:, :q_width]
            kv_ref[...] = product[:, q_width:]

    first = pl.BlockSpec((1, width, length), lambda h, k, at: (jnp.where(h == 0, k, 3), 0, 0))
    second = pl.BlockSpec((1, width, length), lambda h, k, at: (jnp.where(h == 0, 0, k), 0, 0))

    def side(h, at):
        return jnp.where(h == 0, at[CORE], 1 - at[CORE])

    return call(
        kernel,
        "q_gradient",
        order,
        [(a, first) for a in own]
        + [(a, second) for a in other]
        + [whole(a) for a in rows]
        + [(gain_column, pl.BlockSpec((width, 1), lambda h, k, at: (side(h, at), 0)))],
        [
            (
                shape((2 * width, size), f32),
                pl.BlockSpec((width, size), lambda h, k, at: (side(h, at), 0)),
            )
            for size in (q_width, total - q_width)
        ],
        grid=(2, 4),
        scratch=[pltpu.VMEM((width, total), f32)],
    )


def near(parts):
    return {k: partner(parts[k], "dp", 2 * k) for k in (1, 3)}


def far(parts):
    return {2: partner(parts[2], "dp", 4)}


def in_order(*found):
    merged = {}
    for part in found:
        merged.update(part)
    return [merged[k] for k in sorted(merged)]


def split_x(name, order, parts):
    def plan(at_ref, ins, outs):
        pairs = []
        for k, ref in enumerate(ins):
            pairs.append((ref.at[at_ref[XL]], outs[0].at[k]))
            pairs.append((ref.at[1 - at_ref[XL]], outs[1].at[k]))
        return pairs

    dims = (len(parts),) + parts[0].shape[1:]
    return move(name, order, parts, [shape(dims)] * 2, plan)


def rotary(length, head):
    freq = theta ** (-(np.arange(head // 2, dtype=np.float64) * 2.0 / head))
    angle = np.arange(length, dtype=np.float64)[:, None] * freq[None, :]
    cosine, sine = np.cos(angle), np.sin(angle)
    return (
        np.concatenate([cosine, cosine], 1).astype(np.float32),
        np.concatenate([-sine, sine], 1).astype(np.float32),
    )


def on_device(tokens, gain, q_weight, kv_weight, o_weight, out_grad):
    t_at = lax.axis_index("tensor")
    dp_at = lax.axis_index("dp")
    at = jnp.stack(
        [t_at, t_at // 2, t_at % 2, t_at // 4, t_at // 2 % 2, dp_at // 2, dp_at % 2]
    ).astype(jnp.int32)
    order = Order(at)
    length, width = tokens.shape[1:]
    q_width, head = q_weight.shape[1], kv_weight.shape[1]
    tables = [jnp.asarray(table) for table in rotary(length, head)]
    gain_float = gain.astype(f32)
    gain_row = gain_float[None, :]
    gain_column = lax.dynamic_slice_in_dim(gain_float, dp_at * 2 * width, 2 * width)[:, None]

    def y_near(parts):
        return {k: partner(parts[k], "tensor", 4 * k) for k in (1, 3)}

    def y_far(parts):
        return {2: partner(parts[2], "tensor", 8)}

    shard, cot = tokens[0], out_grad[0]
    shards = {0: shard, 1: partner(shard, "tensor", 2)}
    for j in (2, 6, 4):
        shards[j] = partner(shard, "tensor", 2 * j)
    for j in (2, 6, 4):
        shards[j ^ 1] = partner(shards[1], "tensor", 2 * j)
    cot_other = partner(cot, "tensor", 2)
    own, cot_pair = stack("stack_tokens", order, [shards[j] for j in range(8)], [cot, cot_other])
    other = partner(own, "tensor", 1)
    cot_near = y_near([cot_pair] * 4)

    blocks = pick_tokens(order, own)
    token_near = near(blocks)
    normed, inverse, own_tokens = norm(order, gain_row, own, other)
    order.wait(*cot_near.values())
    rot, kv_own = project(order, normed, q_weight, kv_weight, tables)
    cot_far = y_far([cot_pair] * 4)
    kv_other = partner(kv_own, "tensor", 1)
    order.wait(*token_near.values())
    attn, probs, attn_turned = attend(order, rot, kv_own, kv_other)
    token_far = far(blocks)
    send, keep = mix(order, attn, o_weight)
    arrived = partner(send, "tensor", 1)

    (cot_own,) = stack("stack_cot", order, in_order({0: cot_pair}, cot_near, cot_far))
    cot_other = partner(cot_own, "tensor", 1)

    def cot_plan(at_ref, ins, outs):
        return [
            (ins[0].at[at_ref[CHIP] ^ (2 * (at_ref[Z] ^ k) + x)], outs[k].at[x])
            for k in range(4)
            for x in range(2)
        ]

    cot_blocks = move(
        "pick_cot", order, [cot_own], [shape((2, length, width))] * 4, cot_plan
    )
    b_near = near(cot_blocks)
    a_keep, a_send = split_x(
        "split_tokens", order, in_order({0: blocks[0]}, token_near, token_far)
    )
    a_cross = partner(a_send, "dp", 1)
    out_parts = pair_sum(order, keep, arrived, 4, Y)
    out_near = y_near(out_parts)

    dattn, own_cot = out_gradient(order, cot_own, cot_other, o_weight)
    order.wait(*b_near.values())
    dq, dkv_keep, send = attend_gradient(order, dattn, probs, rot, kv_own, kv_other, tables)
    b_far = far(cot_blocks)
    arrived = partner(send, "tensor", 1)
    order.wait(*out_near.values())
    dqkv, scaled = join_gradient(order, dq, dkv_keep, arrived, inverse, tables)
    scaled_other = partner(scaled, "dp", 1)
    out_far = y_far(out_parts)
    attn_near = near([attn_turned] * 4)
    order.wait(a_cross)

    send, keep, gain_part = norm_gradient(order, dqkv, q_weight, kv_weight, normed, gain_row)
    arrived = partner(send, "tensor", 1)
    order.wait(*attn_near.values())
    (pair,) = stack("stack_dqkv", order, [scaled, scaled_other])
    dqkv_near = near([pair] * 4)
    out_keep, out_send = ring_sum(order, in_order({0: out_parts[0]}, out_near, out_far))
    out_arrived = partner(out_send, "tensor", 2)
    x_parts = pair_sum(order, keep, arrived, 4, Y)
    x_near = y_near(x_parts)

    gain_part = lax.all_to_all(gain_part, "dp", 0, 0, tiled=True)
    gain_part = jnp.broadcast_to(jnp.sum(gain_part, axis=0)[None], (16, 1, 2 * width))
    gain_grad = jnp.sum(lax.all_to_all(gain_part, "tensor", 0, 0, tiled=True), axis=0)
    result = (own_tokens.astype(f32) + (out_keep + out_arrived.astype(f32))).astype(bf16)

    attn_far = far([attn_turned] * 4)
    (b_own,) = stack("stack_b", order, in_order({0: cot_blocks[0]}, b_near, b_far))
    b_other = partner(b_own, "tensor", 1)
    a_other = [partner(a, "tensor", 1) for a in (a_keep, a_cross)]
    order.wait(*dqkv_near.values())
    send, keep = out_terms(
        order, b_own, b_other, in_order({0: attn_turned}, attn_near, attn_far)
    )
    dqkv_far = far([pair] * 4)
    o_arrived = partner(send, "dp", 1)
    x_far = y_far(x_parts)
    x_keep, x_send = ring_sum(order, in_order({0: x_parts[0]}, x_near, x_far))
    x_arrived = partner(x_send, "tensor", 2)
    o_grad = keep + o_arrived.astype(f32)

    q_grad, kv_grad = q_gradient(
        order,
        [a_keep, a_cross],
        a_other,
        in_order({0: pair}, dqkv_near, dqkv_far),
        gain_column,
        q_width,
    )
    x_grad = input_gradient(order, x_keep, x_arrived, own_tokens, inverse, own_cot, gain_row)
    return (result[None], x_grad[None], gain_grad.reshape(-1), q_grad, kv_grad, o_grad)


def solution(mesh):
    in_specs = (
        P("dp", None, "tensor"),
        P(),
        P(None, "tensor"),
        P(None, "tensor"),
        P("tensor", None),
        P("dp", None, "tensor"),
    )
    out_specs = (
        P("dp", "tensor", None),
        P("dp", "tensor", None),
        P("dp"),
        P("dp", "tensor"),
        P("dp", "tensor"),
        P("tensor", "dp"),
    )
    return jax.shard_map(
        on_device, mesh=mesh, in_specs=in_specs, out_specs=out_specs, check_vma=False
    )
```

```python
import jax
import jax.numpy as jnp
import numpy as np
from jax import lax
from jax.experimental import pallas as pl
from jax.experimental.pallas import tpu as pltpu
from jax.sharding import PartitionSpec as P

epsilon = 1e-05
theta = 500000.0
f32 = jnp.float32
bf16 = jnp.bfloat16
VMEM = 20 * 1024 * 1024
ANY = pl.BlockSpec(memory_space=pl.ANY)
T, CHIP, CORE, Y, X, Z, XL = range(7)


def partner(array, axis, bits):
    return lax.ppermute(array, axis, [(i, i ^ bits) for i in range(lax.axis_size(axis))])


class Order:
    def __init__(self, at):
        self.at, self.last = at, []

    def wait(self, *arrays):
        self.last = self.last + list(arrays)


def call(kernel, name, order, operands, outputs, grid=(1,), scratch=()):
    arrays = [array for array, _ in operands]
    after = [a for a in order.last if not any(a is b for b in arrays)]
    count, extra = len(arrays), len(after)

    def body(at_ref, *refs):
        kernel(at_ref, *refs[:count], *refs[count + extra :])

    results = pl.pallas_call(
        body,
        grid_spec=pltpu.PrefetchScalarGridSpec(
            num_scalar_prefetch=1,
            grid=grid,
            in_specs=[spec for _, spec in operands] + [ANY] * extra,
            out_specs=[spec for _, spec in outputs],
            scratch_shapes=list(scratch),
        ),
        out_shape=[shape for shape, _ in outputs],
        compiler_params=pltpu.CompilerParams(vmem_limit_bytes=VMEM),
        cost_estimate=pl.CostEstimate(flops=1, bytes_accessed=1, transcendentals=0),
        name=name,
    )(order.at, *arrays, *after)
    order.last = [results[0]]
    return results


def whole(array):
    rank = len(array.shape)
    return (array, pl.BlockSpec(tuple(array.shape), lambda *_: (0,) * rank))


def shape(dims, dtype=bf16):
    return jax.ShapeDtypeStruct(tuple(dims), dtype)


def nt(left, right):
    return lax.dot_general(left, right, (((1,), (1,)), ((), ())), preferred_element_type=f32)


def tn(left, right):
    return lax.dot_general(left, right, (((0,), (0,)), ((), ())), preferred_element_type=f32)


def nn(left, right):
    return jnp.dot(left, right, preferred_element_type=f32)


def move(name, order, sources, out_shapes, plan):
    count, outs_count = len(sources), len(out_shapes)

    def kernel(at_ref, *refs):
        ins, outs = refs[:count], refs[count : count + outs_count]
        held, sems, out_sems = refs[count + outs_count : -2], refs[-2], refs[-1]
        copies = [
            pltpu.make_async_copy(source, target, sems.at[number])
            for number, (source, target) in enumerate(plan(at_ref, ins, held))
        ]
        for copy in copies:
            copy.start()
        for copy in copies:
            copy.wait()
        copies = [
            pltpu.make_async_copy(source, target, out_sems.at[number])
            for number, (source, target) in enumerate(zip(held, outs))
        ]
        for copy in copies:
            copy.start()
        for copy in copies:
            copy.wait()

    return call(
        kernel,
        name,
        order,
        [(source, ANY) for source in sources],
        [(s, ANY) for s in out_shapes],
        scratch=[pltpu.VMEM(s.shape, s.dtype) for s in out_shapes]
        + [pltpu.SemaphoreType.DMA((16,))] * 2,
    )


def stack(name, order, *groups):
    groups = [[p if p.ndim == 3 else p[None] for p in group] for group in groups]
    sources = [p for group in groups for p in group]

    def plan(at_ref, ins, outs):
        pairs, number = [], 0
        for group, out in zip(groups, outs):
            row = 0
            for p in group:
                pairs.append((ins[number], out.at[pl.ds(row, p.shape[0])]))
                row += p.shape[0]
                number += 1
        return pairs

    outs = [shape((sum(p.shape[0] for p in g),) + g[0].shape[1:], g[0].dtype) for g in groups]
    return move(name, order, sources, outs, plan)


def norm(order, gain_row, own, other):
    chips, length, width = own.shape
    tile = 64
    full = 2 * chips * width

    def kernel(at_ref, gain_ref, own_ref, other_ref, normed_ref, inverse_ref, rows_ref):
        chip, core = at_ref[CHIP], at_ref[CORE]

        def columns(pair, half):
            return pl.ds(pl.multiple_of((2 * pair + half) * width, width), width)

        @pl.loop(0, tile // 16)
        def _(step):
            here = pl.ds(pl.multiple_of(step * 16, 16), 16)
            squares = jnp.zeros((16, width), f32)
            for j in range(chips):
                for ref in (own_ref, other_ref):
                    value = ref[j, here, :].astype(f32)
                    squares += value * value
            mean = jnp.sum(squares, axis=-1, keepdims=True) / full
            inverse = lax.rsqrt(mean + epsilon)
            inverse_ref[here, :] = inverse
            for j in range(chips):
                for ref, half in ((own_ref, core), (other_ref, 1 - core)):
                    place = columns(chip ^ j, half)
                    value = ref[j, here, :].astype(f32)
                    normed_ref[here, place] = (value * inverse * gain_ref[:, place]).astype(bf16)

            @pl.when(pl.program_id(0) * (tile // 16) + step == at_ref[T])
            def _():
                for j in range(chips):
                    for ref, half in ((own_ref, core), (other_ref, 1 - core)):
                        rows_ref[:, columns(chip ^ j, half)] = ref[j, here, :]

    block = pl.BlockSpec((chips, tile, width), lambda i, at: (0, i, 0))
    return call(
        kernel,
        "norm",
        order,
        [whole(gain_row), (own, block), (other, block)],
        [
            (shape((length, full)), pl.BlockSpec((tile, full), lambda i, at: (i, 0))),
            (shape((length, 1), f32), pl.BlockSpec((tile, 1), lambda i, at: (i, 0))),
            (shape((16, full)), pl.BlockSpec((16, full), lambda i, at: (0, 0))),
        ],
        grid=(length // tile,),
    )


def pick_tokens(name, order, own, partners, *copied):
    chips, length, width = own.shape
    count = len(partners)

    def kernel(at_ref, own_ref, *refs):
        ins, out, copies = refs[: len(copied)], refs[len(copied) :][:count], refs[len(copied) + count :]
        for number, k in enumerate(partners):
            for x in range(2):
                out[number][x] = own_ref[at_ref[CHIP] ^ (2 * (at_ref[Z] ^ k) + x)].T
        for source, target in zip(ins, copies):
            target[...] = source[...]

    return call(
        kernel,
        name,
        order,
        [whole(own)] + [whole(c) for c in copied],
        [whole_out((2, width, length))] * count + [whole_out(c.shape) for c in copied],
    )


def turned(value, cos_ref, sin_ref, direction):
    swapped = pltpu.roll(value, value.shape[-1] // 2, 1)
    return value * cos_ref[...] + swapped * (sin_ref[...] * direction)


def project(order, normed, q_weight, kv_weight, tables):
    length, full = normed.shape
    q_width, head = q_weight.shape[1], kv_weight.shape[1]
    tile = 1024

    def kernel(at_ref, x_ref, q_ref, kv_ref, cos_ref, sin_ref, rot_ref, own_ref, qacc, kvacc):
        step = pl.program_id(0)

        @pl.when(step == 0)
        def _():
            qacc[...] = jnp.zeros_like(qacc)
            kvacc[...] = jnp.zeros_like(kvacc)

        qacc[...] += nn(x_ref[...], q_ref[...])
        kvacc[...] += nn(x_ref[...], kv_ref[...])

        @pl.when(step == pl.num_programs(0) - 1)
        def _():
            for h in range(q_width // head):
                place = slice(h * head, (h + 1) * head)
                rot_ref[:, place] = turned(qacc[:, place], cos_ref, sin_ref, 1.0).astype(bf16)
            plain = kvacc[...]
            rotated = turned(plain, cos_ref, sin_ref, 1.0)
            own_ref[...] = jnp.where(at_ref[CORE] == 0, rotated, plain).astype(bf16)

    return call(
        kernel,
        "project",
        order,
        [
            (normed, pl.BlockSpec((length, tile), lambda i, at: (0, i))),
            (q_weight, pl.BlockSpec((tile, q_width), lambda i, at: (i, 0))),
            (kv_weight, pl.BlockSpec((tile, head), lambda i, at: (i, 0))),
            whole(tables[0]),
            whole(tables[1]),
        ],
        [whole_out((length, q_width)), whole_out((length, head))],
        grid=(full // tile,),
        scratch=[pltpu.VMEM((length, q_width), f32), pltpu.VMEM((length, head), f32)],
    )


def whole_out(dims, dtype=bf16):
    return whole(shape(dims, dtype))


def attend(order, rot, own, other):
    length, q_width = rot.shape
    head = own.shape[1]
    heads = q_width // head
    scale = head ** (-0.5)

    def kernel(at_ref, rot_ref, own_ref, other_ref, attn_ref, probs_ref):
        even = at_ref[CORE] == 0
        key = jnp.where(even, own_ref[...], other_ref[...])
        value = jnp.where(even, other_ref[...], own_ref[...])
        row = lax.broadcasted_iota(jnp.int32, (length, length), 0)
        column = lax.broadcasted_iota(jnp.int32, (length, length), 1)
        for h in range(heads):
            place = slice(h * head, (h + 1) * head)
            scores = jnp.where(row >= column, nt(rot_ref[:, place], key) * scale, -1e30)
            expo = jnp.exp(scores - jnp.max(scores, axis=-1, keepdims=True))
            probs = expo / jnp.sum(expo, axis=-1, keepdims=True)
            probs_ref[h] = probs
            attn_ref[:, place] = nn(probs.astype(bf16), value).astype(bf16)

    return call(
        kernel,
        "attend",
        order,
        [whole(rot), whole(own), whole(other)],
        [
            whole_out((length, q_width)),
            whole_out((heads, length, length), f32),
        ],
    )


def split_rows(at_ref, product, rows_ref, send_ref, keep_ref):
    rows_ref[...] = product.reshape(rows_ref.shape)
    send_ref[...] = rows_ref[:, 1 - at_ref[CORE]].astype(bf16)
    keep_ref[...] = rows_ref[:, at_ref[CORE]].astype(bf16)


def mix(order, attn, o_weight):
    length, q_width = attn.shape
    full = o_weight.shape[1]
    tile = 1024

    def kernel(at_ref, attn_ref, w_ref, send_ref, keep_ref, rows_ref):
        split_rows(at_ref, nn(attn_ref[...], w_ref[...]), rows_ref, send_ref, keep_ref)

    out = (shape((length // 32, 16, full)), pl.BlockSpec((length // 32, 16, tile), lambda i, at: (0, 0, i)))
    return call(
        kernel,
        "mix",
        order,
        [whole(attn), (o_weight, pl.BlockSpec((q_width, tile), lambda i, at: (0, i)))],
        [out, out],
        grid=(full // tile,),
        scratch=[pltpu.VMEM((length // 32, 2, 16, tile), f32)],
    )


def pair_sum(order, keep, arrived, groups, index):
    chips, _, full = keep.shape
    each = chips // groups
    tile = 2048

    def kernel(at_ref, keep_ref, arrived_ref, *out):
        for k in range(groups):
            here = pl.ds((at_ref[index] ^ k) * each, each) if groups > 1 else slice(None)
            out[k][...] = (keep_ref[here].astype(f32) + arrived_ref[here].astype(f32)).astype(bf16)

    block = pl.BlockSpec((chips, 16, tile), lambda i, at: (0, 0, i))
    out = (shape((each, 16, full)), pl.BlockSpec((each, 16, tile), lambda i, at: (0, 0, i)))
    return call(
        kernel,
        "pair_sum",
        order,
        [(keep, block), (arrived, block)],
        [out] * groups,
        grid=(full // tile,),
    )


def ring_sum(order, parts):
    _, _, full = parts[0].shape
    tile = 2048

    def kernel(at_ref, *refs):
        parts, keep_ref, send_ref = refs[:4], refs[4], refs[5]
        for target, x in ((keep_ref, at_ref[X]), (send_ref, 1 - at_ref[X])):
            total = parts[0][x].astype(f32)
            for part in parts[1:]:
                total += part[x].astype(f32)
            target[...] = total.astype(target.dtype)

    block = pl.BlockSpec((2, 16, tile), lambda i, at: (0, 0, i))
    out = pl.BlockSpec((16, tile), lambda i, at: (0, i))
    return call(
        kernel,
        "ring_sum",
        order,
        [(part, block) for part in parts],
        [(shape((16, full), f32), out), (shape((16, full)), out)],
        grid=(full // tile,),
    )


def out_gradient(order, own, other, o_weight):
    chips, length, width = own.shape
    q_width, full = o_weight.shape

    def kernel(at_ref, own_ref, other_ref, w_ref, dattn_ref, rows_ref, acc):
        step = pl.program_id(0)
        core = at_ref[CORE]

        @pl.when(step == 0)
        def _():
            acc[...] = jnp.zeros_like(acc)

        mine = pl.ds(pl.multiple_of(at_ref[T] * 16, 16), 16)
        for ref, half in ((own_ref, core), (other_ref, 1 - core)):
            place = pl.ds(pl.multiple_of(half * width, width), width)
            acc[...] += nt(ref[0], w_ref[:, place])
            rows_ref[:, place] = ref[0, mine, :]

        @pl.when(step == pl.num_programs(0) - 1)
        def _():
            dattn_ref[...] = acc[...].astype(bf16)

    block = pl.BlockSpec((1, length, width), lambda i, at: (i, 0, 0))
    return call(
        kernel,
        "out_gradient",
        order,
        [
            (own, block),
            (other, block),
            (o_weight, pl.BlockSpec((q_width, 2 * width), lambda i, at: (0, at[CHIP] ^ i))),
        ],
        [
            whole_out((length, q_width)),
            (shape((16, full)), pl.BlockSpec((16, 2 * width), lambda i, at: (0, at[CHIP] ^ i))),
        ],
        grid=(chips,),
        scratch=[pltpu.VMEM((length, q_width), f32)],
    )


def attend_gradient(order, dattn, probs, rot, own, other, tables):
    length, q_width = rot.shape
    head = own.shape[1]
    scale = head ** (-0.5)

    def kernel(
        at_ref, dattn_ref, probs_ref, rot_ref, own_ref, other_ref, cos_ref, sin_ref,
        dq_ref, keep_ref, send_ref,
    ):
        even = at_ref[CORE] == 0
        key = jnp.where(even, own_ref[...], other_ref[...])
        value = jnp.where(even, other_ref[...], own_ref[...])
        dkey = jnp.zeros((length, head), f32)
        dvalue = jnp.zeros((length, head), f32)
        for h in range(q_width // head):
            place = slice(h * head, (h + 1) * head)
            probs = probs_ref[h]
            dattn = dattn_ref[:, place]
            dprobs = nt(dattn, value)
            delta = jnp.sum(dprobs * probs, axis=-1, keepdims=True)
            dscores = (probs * (dprobs - delta) * scale).astype(bf16)
            dq_ref[:, place] = turned(nn(dscores, key), cos_ref, sin_ref, -1.0).astype(bf16)
            dkey += tn(dscores, rot_ref[:, place])
            dvalue += tn(probs.astype(bf16), dattn)
        keep_ref[...] = jnp.where(even, dkey, dvalue)
        send_ref[...] = jnp.where(even, dvalue, dkey).astype(bf16)

    return call(
        kernel,
        "attend_gradient",
        order,
        [whole(a) for a in (dattn, probs, rot, own, other, *tables)],
        [whole_out((length, q_width)), whole_out((length, head), f32), whole_out((length, head))],
    )


def join_gradient(order, dq, keep, arrived, inverse, tables):
    length, q_width = dq.shape
    head = keep.shape[1]

    def kernel(
        at_ref, dq_ref, keep_ref, arrived_ref, inverse_ref, cos_ref, sin_ref, out_ref, scaled_ref
    ):
        inverse = inverse_ref[...]
        dq = dq_ref[...]
        out_ref[:, :q_width] = dq
        scaled_ref[:, :q_width] = (dq.astype(f32) * inverse).astype(bf16)
        plain = keep_ref[...] + arrived_ref[...].astype(f32)
        back = turned(plain, cos_ref, sin_ref, -1.0)
        own = jnp.where(at_ref[CORE] == 0, back, plain).astype(bf16)
        out_ref[:, q_width:] = own
        scaled_ref[:, q_width:] = (own.astype(f32) * inverse).astype(bf16)

    return call(
        kernel,
        "join_gradient",
        order,
        [whole(a) for a in (dq, keep, arrived, inverse, *tables)],
        [whole_out((length, q_width + head))] * 2,
    )


def norm_gradient(order, dqkv, q_weight, kv_weight, normed, gain_row):
    length, full = normed.shape
    q_width, head = q_weight.shape[1], kv_weight.shape[1]
    tile = 1024

    def kernel(
        at_ref, d_ref, q_ref, kv_ref, normed_ref, gain_ref, send_ref, keep_ref, part_ref, rows_ref
    ):
        product = nt(d_ref[:, :q_width], q_ref[...]) + nt(d_ref[:, q_width:], kv_ref[...])
        part = jnp.sum(product * normed_ref[...].astype(f32), axis=0, keepdims=True)
        part_ref[0] = part / gain_ref[...]
        split_rows(at_ref, product, rows_ref, send_ref, keep_ref)

    out = (shape((length // 32, 16, full)), pl.BlockSpec((length // 32, 16, tile), lambda i, at: (0, 0, i)))
    return call(
        kernel,
        "norm_gradient",
        order,
        [
            whole(dqkv),
            (q_weight, pl.BlockSpec((tile, q_width), lambda i, at: (i, 0))),
            (kv_weight, pl.BlockSpec((tile, head), lambda i, at: (i, 0))),
            (normed, pl.BlockSpec((length, tile), lambda i, at: (0, i))),
            (gain_row, pl.BlockSpec((1, tile), lambda i, at: (0, i))),
        ],
        [out, out, (shape((full // tile, 1, tile), f32), pl.BlockSpec((1, 1, tile), lambda i, at: (i, 0, 0)))],
        grid=(full // tile,),
        scratch=[pltpu.VMEM((length // 32, 2, 16, tile), f32)],
    )


def input_gradient(order, keep, arrived, tokens, inverse, cotangent, gain_row):
    rows, full = tokens.shape

    def kernel(
        at_ref, keep_ref, arrived_ref, tokens_ref, inverse_ref, cot_ref, gain_ref, out_ref,
        xhat_ref, scaled_ref,
    ):
        inverse = inverse_ref[pl.ds(pl.multiple_of(at_ref[T] * 16, 16), 16), :]
        tile = 1024
        dots = jnp.zeros((rows, tile), f32)
        for i in range(full // tile):
            place = slice(i * tile, (i + 1) * tile)
            total = keep_ref[:, place] + arrived_ref[:, place].astype(f32)
            xhat = tokens_ref[:, place].astype(f32) * inverse
            scaled = total * gain_ref[:, place]
            xhat_ref[:, place] = xhat
            scaled_ref[:, place] = scaled
            dots += scaled * xhat
        mean = jnp.sum(dots, axis=-1, keepdims=True) / full
        for i in range(full // tile):
            place = slice(i * tile, (i + 1) * tile)
            change = inverse * (scaled_ref[:, place] - xhat_ref[:, place] * mean)
            out_ref[:, place] = (cot_ref[:, place].astype(f32) + change).astype(bf16)

    return call(
        kernel,
        "input_gradient",
        order,
        [whole(a) for a in (keep, arrived, tokens, inverse, cotangent, gain_row)],
        [whole_out((rows, full))],
        scratch=[pltpu.VMEM((rows, full), f32)] * 2,
    )[0]


def out_terms(order, own, other, rows):
    _, length, width = own.shape
    total = rows.shape[2]

    def kernel(at_ref, own_ref, other_ref, rows_ref, send_ref, keep_ref, acc, turned_ref):
        step = pl.program_id(0)

        @pl.when(step == 0)
        def _():
            for k in range(4):
                turned_ref[k] = rows_ref[k].T

        def add(ref):
            acc[...] = nn(turned_ref[0], ref[0, 0])
            for k in range(1, 4):
                acc[...] += nn(turned_ref[k], ref[k, 0])

        pl.when(step % 2 == 0)(lambda: add(own_ref))
        pl.when(step % 2 == 1)(lambda: add(other_ref))

        @pl.when(step < 2)
        def _():
            send_ref[...] = acc[...].astype(bf16)

        @pl.when(step >= 2)
        def _():
            keep_ref[...] = acc[...]

    def x_of(i, at):
        return jnp.where(i < 2, 1 - at[XL], at[XL])

    def side(half, at):
        return jnp.where(half == 0, at[CORE], 1 - at[CORE])

    block = pl.BlockSpec((4, 1, length, width), lambda i, at: (0, x_of(i, at), 0, 0))
    dims = (4, 2, length, width)
    return call(
        kernel,
        "out_terms",
        order,
        [(own.reshape(dims), block), (other.reshape(dims), block), whole(rows)],
        [
            (
                shape((total, 2 * width)),
                pl.BlockSpec((total, width), lambda i, at: (0, side(jnp.minimum(i, 1), at))),
            ),
            (
                shape((total, 2 * width), f32),
                pl.BlockSpec((total, width), lambda i, at: (0, side(jnp.maximum(i - 2, 0), at))),
            ),
        ],
        grid=(4,),
        scratch=[pltpu.VMEM((total, width), f32), pltpu.VMEM((4, total, length), bf16)],
    )


def q_gradient(order, own, other, rows, gain_column, q_width):
    _, width, length = own[0].shape
    total = rows[0].shape[2]

    def kernel(at_ref, *refs):
        blocks, row_refs, gain_ref, q_ref, kv_ref, acc = refs[:4], refs[4:8], *refs[8:]
        half, k = pl.program_id(0), pl.program_id(1)

        def add(pair):
            for number in range(4):

                @pl.when(k == number)
                def _():
                    term = nn(pair[0][0], row_refs[number][0]) + nn(pair[1][0], row_refs[number][1])
                    if number == 0:
                        acc[...] = term
                    else:
                        acc[...] += term

        pl.when(half == 0)(lambda: add(blocks[:2]))
        pl.when(half == 1)(lambda: add(blocks[2:]))

        @pl.when(k == 3)
        def _():
            product = acc[...] * gain_ref[...]
            q_ref[...] = product[:, :q_width]
            kv_ref[...] = product[:, q_width:]

    first = pl.BlockSpec((1, width, length), lambda h, k, at: (jnp.where(h == 0, k, 3), 0, 0))
    second = pl.BlockSpec((1, width, length), lambda h, k, at: (jnp.where(h == 0, 0, k), 0, 0))

    def side(h, at):
        return jnp.where(h == 0, at[CORE], 1 - at[CORE])

    return call(
        kernel,
        "q_gradient",
        order,
        [(a, first) for a in own]
        + [(a, second) for a in other]
        + [whole(a) for a in rows]
        + [(gain_column, pl.BlockSpec((width, 1), lambda h, k, at: (side(h, at), 0)))],
        [
            (
                shape((2 * width, size), f32),
                pl.BlockSpec((width, size), lambda h, k, at: (side(h, at), 0)),
            )
            for size in (q_width, total - q_width)
        ],
        grid=(2, 4),
        scratch=[pltpu.VMEM((width, total), f32)],
    )


def near(parts):
    return {k: partner(parts[k], "dp", 2 * k) for k in (1, 3)}


def far(parts):
    return {2: partner(parts[2], "dp", 4)}


def in_order(*found):
    merged = {}
    for part in found:
        merged.update(part)
    return [merged[k] for k in sorted(merged)]


def split_x(name, order, parts):
    def plan(at_ref, ins, outs):
        pairs = []
        for k, ref in enumerate(ins):
            pairs.append((ref.at[at_ref[XL]], outs[0].at[k]))
            pairs.append((ref.at[1 - at_ref[XL]], outs[1].at[k]))
        return pairs

    dims = (len(parts),) + parts[0].shape[1:]
    return move(name, order, parts, [shape(dims)] * 2, plan)


def stack_b(order, parts):
    _, length, width = parts[0].shape

    def plan(at_ref, ins, outs):
        pairs = [(ref.at[pl.ds(0, 2)], outs[0].at[pl.ds(2 * k, 2)]) for k, ref in enumerate(ins)]
        return pairs + [(ref.at[2], outs[1].at[k]) for k, ref in enumerate(ins)]

    return move(
        "stack_b", order, parts, [shape((8, length, width)), shape((4, length, width))], plan
    )


def rotary(length, head):
    freq = theta ** (-(np.arange(head // 2, dtype=np.float64) * 2.0 / head))
    angle = np.arange(length, dtype=np.float64)[:, None] * freq[None, :]
    cosine, sine = np.cos(angle), np.sin(angle)
    return (
        np.concatenate([cosine, cosine], 1).astype(np.float32),
        np.concatenate([-sine, sine], 1).astype(np.float32),
    )


def on_device(tokens, gain, q_weight, kv_weight, o_weight, out_grad):
    t_at = lax.axis_index("tensor")
    dp_at = lax.axis_index("dp")
    at = jnp.stack(
        [t_at, t_at // 2, t_at % 2, t_at // 4, t_at // 2 % 2, dp_at // 2, dp_at % 2]
    ).astype(jnp.int32)
    order = Order(at)
    length, width = tokens.shape[1:]
    q_width, head = q_weight.shape[1], kv_weight.shape[1]
    tables = [jnp.asarray(table) for table in rotary(length, head)]
    gain_float = gain.astype(f32)
    gain_row = gain_float[None, :]
    gain_column = lax.dynamic_slice_in_dim(gain_float, dp_at * 2 * width, 2 * width)[:, None]

    def y_near(parts):
        return {k: partner(parts[k], "tensor", 4 * k) for k in (1, 3)}

    def y_far(parts):
        return {2: partner(parts[2], "tensor", 8)}

    shard, cot = tokens[0], out_grad[0]
    shards = {0: shard, 1: partner(shard, "tensor", 2)}
    for j in (2, 6, 4):
        shards[j] = partner(shard, "tensor", 2 * j)
    for j in (2, 6, 4):
        shards[j ^ 1] = partner(shards[1], "tensor", 2 * j)
    cot_other = partner(cot, "tensor", 2)
    own, cot_pair = stack("stack_tokens", order, [shards[j] for j in range(8)], [cot, cot_other])
    other = partner(own, "tensor", 1)
    cot_near = y_near([cot_pair] * 4)

    blocks = dict(zip((0, 1, 3), pick_tokens("pick_near", order, own, (0, 1, 3))))
    token_near = near(blocks)
    normed, inverse, own_tokens = norm(order, gain_row, own, other)
    rot, kv_own = project(order, normed, q_weight, kv_weight, tables)
    blocks[2], cot_copy = pick_tokens("pick_far", order, own, (2,), cot_pair)
    cot_far = y_far([cot_copy] * 4)
    kv_other = partner(kv_own, "tensor", 1)
    token_far = far(blocks)
    order.wait(*token_near.values(), *cot_near.values())
    attn, probs = attend(order, rot, kv_own, kv_other)
    send, keep = mix(order, attn, o_weight)
    arrived = partner(send, "tensor", 1)

    order.wait(*token_far.values())
    (cot_own,) = stack("stack_cot", order, in_order({0: cot_pair}, cot_near, cot_far))
    cot_other = partner(cot_own, "tensor", 1)

    def cot_plan(at_ref, ins, outs):
        return [
            (ins[0].at[at_ref[CHIP] ^ (2 * (at_ref[Z] ^ k) + x)], outs[k].at[x])
            for k in range(4)
            for x in range(2)
        ] + [(ins[1], outs[k].at[2]) for k in range(4)]

    cot_blocks = move(
        "pick_cot", order, [cot_own, attn], [shape((3, length, width))] * 4, cot_plan
    )
    b_near = near(cot_blocks)
    a_keep, a_send = split_x(
        "split_tokens", order, in_order({0: blocks[0]}, token_near, token_far)
    )
    a_cross = partner(a_send, "dp", 1)
    out_parts = pair_sum(order, keep, arrived, 4, Y)
    out_near = y_near(out_parts)

    dattn, own_cot = out_gradient(order, cot_own, cot_other, o_weight)
    dq, dkv_keep, send = attend_gradient(order, dattn, probs, rot, kv_own, kv_other, tables)
    b_far = far(cot_blocks)
    arrived = partner(send, "tensor", 1)
    order.wait(*b_near.values(), *out_near.values(), a_cross)
    dqkv, scaled = join_gradient(order, dq, dkv_keep, arrived, inverse, tables)
    scaled_other = partner(scaled, "dp", 1)
    out_far = y_far(out_parts)

    send, keep, gain_part = norm_gradient(order, dqkv, q_weight, kv_weight, normed, gain_row)
    arrived = partner(send, "tensor", 1)
    x_parts = pair_sum(order, keep, arrived, 4, Y)
    x_near = y_near(x_parts)
    gain_part = jnp.sum(lax.all_to_all(gain_part, "dp", 0, 0, tiled=True), axis=0)
    order.wait(*b_far.values(), *out_far.values(), *x_near.values(), gain_part)
    (pair,) = stack("stack_dqkv", order, [scaled, scaled_other])
    dqkv_near = near([pair] * 4)
    (b_own, attn_all) = stack_b(order, in_order({0: cot_blocks[0]}, b_near, b_far))
    b_other = partner(b_own, "tensor", 1)
    gain_part = lax.all_to_all(
        jnp.broadcast_to(gain_part[None], (16, 1, 2 * width)), "tensor", 0, 0, tiled=True
    )
    gain_grad = jnp.sum(gain_part, axis=0)
    x_far = y_far(x_parts)
    order.wait(gain_grad)
    out_keep, out_send = ring_sum(order, in_order({0: out_parts[0]}, out_near, out_far))
    out_arrived = partner(out_send, "tensor", 2)
    a_other = [partner(a, "tensor", 1) for a in (a_keep, a_cross)]
    order.wait(*dqkv_near.values())
    send, keep = out_terms(order, b_own, b_other, attn_all)
    dqkv_far = far([pair] * 4)
    o_arrived = partner(send, "dp", 1)
    result = (own_tokens.astype(f32) + (out_keep + out_arrived.astype(f32))).astype(bf16)

    x_keep, x_send = ring_sum(order, in_order({0: x_parts[0]}, x_near, x_far))
    x_arrived = partner(x_send, "tensor", 2)
    o_grad = keep + o_arrived.astype(f32)

    order.wait(o_arrived)
    q_grad, kv_grad = q_gradient(
        order,
        [a_keep, a_cross],
        a_other,
        in_order({0: pair}, dqkv_near, dqkv_far),
        gain_column,
        q_width,
    )
    x_grad = input_gradient(order, x_keep, x_arrived, own_tokens, inverse, own_cot, gain_row)
    return (result[None], x_grad[None], gain_grad.reshape(-1), q_grad, kv_grad, o_grad)


def solution(mesh):
    in_specs = (
        P("dp", None, "tensor"),
        P(),
        P(None, "tensor"),
        P(None, "tensor"),
        P("tensor", None),
        P("dp", None, "tensor"),
    )
    out_specs = (
        P("dp", "tensor", None),
        P("dp", "tensor", None),
        P("dp"),
        P("dp", "tensor"),
        P("dp", "tensor"),
        P("tensor", "dp"),
    )
    return jax.shard_map(
        on_device, mesh=mesh, in_specs=in_specs, out_specs=out_specs, check_vma=False
    )
```

```python
import jax
import jax.numpy as jnp
import numpy as np
from jax import lax
from jax.experimental import pallas as pl
from jax.experimental.pallas import tpu as pltpu
from jax.sharding import PartitionSpec as P

epsilon = 1e-05
theta = 500000.0
f32 = jnp.float32
bf16 = jnp.bfloat16
VMEM = 16 * 1024 * 1024
LATE = 58 * 1024 * 1024
ANY = pl.BlockSpec(memory_space=pl.ANY)
T, CHIP, CORE, Y, X, Z, XL = range(7)


def partner(array, axis, bits):
    return lax.ppermute(array, axis, [(i, i ^ bits) for i in range(lax.axis_size(axis))])


class Order:
    def __init__(self, at):
        self.at, self.last, self.vmem = at, [], VMEM

    def wait(self, *arrays):
        self.last = self.last + list(arrays)


def call(kernel, name, order, operands, outputs, grid=(1,), scratch=()):
    arrays = [array for array, _ in operands]
    after = order.last
    count, extra, results = len(arrays), len(after), len(outputs)

    def body(at_ref, *refs):
        outs = refs[count + extra :]
        outs[results][...] = jnp.zeros_like(outs[results])
        kernel(at_ref, *refs[:count], *outs[:results], *outs[results + 1 :])

    outputs = outputs + [whole_out((8, 128), f32)]

    results = pl.pallas_call(
        body,
        grid_spec=pltpu.PrefetchScalarGridSpec(
            num_scalar_prefetch=1,
            grid=grid,
            in_specs=[spec for _, spec in operands] + [ANY] * extra,
            out_specs=[spec for _, spec in outputs],
            scratch_shapes=list(scratch),
        ),
        out_shape=[shape for shape, _ in outputs],
        compiler_params=pltpu.CompilerParams(vmem_limit_bytes=order.vmem),
        cost_estimate=pl.CostEstimate(flops=1, bytes_accessed=1, transcendentals=0),
        name=name,
    )(order.at, *arrays, *after)
    results = list(results)
    order.last = [results.pop()]
    return results


def whole(array):
    rank = len(array.shape)
    return (array, pl.BlockSpec(tuple(array.shape), lambda *_: (0,) * rank))


def shape(dims, dtype=bf16):
    return jax.ShapeDtypeStruct(tuple(dims), dtype)


def nt(left, right):
    return lax.dot_general(left, right, (((1,), (1,)), ((), ())), preferred_element_type=f32)


def tn(left, right):
    return lax.dot_general(left, right, (((0,), (0,)), ((), ())), preferred_element_type=f32)


def nn(left, right):
    return jnp.dot(left, right, preferred_element_type=f32)


def move(name, order, sources, out_shapes, plan):
    count, outs_count = len(sources), len(out_shapes)

    def kernel(at_ref, *refs):
        ins, outs = refs[:count], refs[count : count + outs_count]
        held, sems, out_sems = refs[count + outs_count : -2], refs[-2], refs[-1]
        copies = [
            pltpu.make_async_copy(source, target, sems.at[number])
            for number, (source, target) in enumerate(plan(at_ref, ins, held))
        ]
        for copy in copies:
            copy.start()
        for copy in copies:
            copy.wait()
        copies = [
            pltpu.make_async_copy(source, target, out_sems.at[number])
            for number, (source, target) in enumerate(zip(held, outs))
        ]
        for copy in copies:
            copy.start()
        for copy in copies:
            copy.wait()

    return call(
        kernel,
        name,
        order,
        [(source, ANY) for source in sources],
        [(s, ANY) for s in out_shapes],
        scratch=[pltpu.VMEM(s.shape, s.dtype) for s in out_shapes]
        + [pltpu.SemaphoreType.DMA((16,))] * 2,
    )


def stack(name, order, *groups):
    groups = [[p if p.ndim == 3 else p[None] for p in group] for group in groups]
    sources = [p for group in groups for p in group]

    def plan(at_ref, ins, outs):
        pairs, number = [], 0
        for group, out in zip(groups, outs):
            row = 0
            for p in group:
                pairs.append((ins[number], out.at[pl.ds(row, p.shape[0])]))
                row += p.shape[0]
                number += 1
        return pairs

    outs = [shape((sum(p.shape[0] for p in g),) + g[0].shape[1:], g[0].dtype) for g in groups]
    return move(name, order, sources, outs, plan)


def norm(order, gain_row, own, other):
    chips, length, width = own.shape
    tile = 64
    full = 2 * chips * width

    def kernel(at_ref, gain_ref, own_ref, other_ref, normed_ref, inverse_ref, rows_ref):
        chip, core = at_ref[CHIP], at_ref[CORE]

        def columns(pair, half):
            return pl.ds(pl.multiple_of((2 * pair + half) * width, width), width)

        @pl.loop(0, tile // 16)
        def _(step):
            here = pl.ds(pl.multiple_of(step * 16, 16), 16)
            squares = jnp.zeros((16, width), f32)
            for j in range(chips):
                for ref in (own_ref, other_ref):
                    value = ref[j, here, :].astype(f32)
                    squares += value * value
            mean = jnp.sum(squares, axis=-1, keepdims=True) / full
            inverse = lax.rsqrt(mean + epsilon)
            inverse_ref[here, :] = inverse
            for j in range(chips):
                for ref, half in ((own_ref, core), (other_ref, 1 - core)):
                    place = columns(chip ^ j, half)
                    value = ref[j, here, :].astype(f32)
                    normed_ref[here, place] = (value * inverse * gain_ref[:, place]).astype(bf16)

            @pl.when(pl.program_id(0) * (tile // 16) + step == at_ref[T])
            def _():
                for j in range(chips):
                    for ref, half in ((own_ref, core), (other_ref, 1 - core)):
                        rows_ref[:, columns(chip ^ j, half)] = ref[j, here, :]

    block = pl.BlockSpec((chips, tile, width), lambda i, at: (0, i, 0))
    return call(
        kernel,
        "norm",
        order,
        [whole(gain_row), (own, block), (other, block)],
        [
            (shape((length, full)), pl.BlockSpec((tile, full), lambda i, at: (i, 0))),
            (shape((length, 1), f32), pl.BlockSpec((tile, 1), lambda i, at: (i, 0))),
            (shape((16, full)), pl.BlockSpec((16, full), lambda i, at: (0, 0))),
        ],
        grid=(length // tile,),
    )


def pick_tokens(name, order, own, partners, *copied):
    chips, length, width = own.shape
    count = len(partners)

    def kernel(at_ref, own_ref, *refs):
        ins, out, copies = refs[: len(copied)], refs[len(copied) :][:count], refs[len(copied) + count :]
        for number, k in enumerate(partners):
            for x in range(2):
                out[number][x] = own_ref[at_ref[CHIP] ^ (2 * (at_ref[Z] ^ k) + x)].T
        for source, target in zip(ins, copies):
            target[...] = source[...]

    return call(
        kernel,
        name,
        order,
        [whole(own)] + [whole(c) for c in copied],
        [whole_out((2, width, length))] * count + [whole_out(c.shape) for c in copied],
    )


def turned(value, cos_ref, sin_ref, direction):
    swapped = pltpu.roll(value, value.shape[-1] // 2, 1)
    return value * cos_ref[...] + swapped * (sin_ref[...] * direction)


def project(order, normed, q_weight, kv_weight, tables):
    length, full = normed.shape
    q_width, head = q_weight.shape[1], kv_weight.shape[1]
    tile = 1024

    def kernel(at_ref, x_ref, q_ref, kv_ref, cos_ref, sin_ref, rot_ref, own_ref, qacc, kvacc):
        step = pl.program_id(0)

        @pl.when(step == 0)
        def _():
            qacc[...] = jnp.zeros_like(qacc)
            kvacc[...] = jnp.zeros_like(kvacc)

        qacc[...] += nn(x_ref[...], q_ref[...])
        kvacc[...] += nn(x_ref[...], kv_ref[...])

        @pl.when(step == pl.num_programs(0) - 1)
        def _():
            for h in range(q_width // head):
                place = slice(h * head, (h + 1) * head)
                rot_ref[:, place] = turned(qacc[:, place], cos_ref, sin_ref, 1.0).astype(bf16)
            plain = kvacc[...]
            rotated = turned(plain, cos_ref, sin_ref, 1.0)
            own_ref[...] = jnp.where(at_ref[CORE] == 0, rotated, plain).astype(bf16)

    return call(
        kernel,
        "project",
        order,
        [
            (normed, pl.BlockSpec((length, tile), lambda i, at: (0, i))),
            (q_weight, pl.BlockSpec((tile, q_width), lambda i, at: (i, 0))),
            (kv_weight, pl.BlockSpec((tile, head), lambda i, at: (i, 0))),
            whole(tables[0]),
            whole(tables[1]),
        ],
        [whole_out((length, q_width)), whole_out((length, head))],
        grid=(full // tile,),
        scratch=[pltpu.VMEM((length, q_width), f32), pltpu.VMEM((length, head), f32)],
    )


def whole_out(dims, dtype=bf16):
    return whole(shape(dims, dtype))


def attend(order, rot, own, other):
    length, q_width = rot.shape
    head = own.shape[1]
    heads = q_width // head
    scale = head ** (-0.5)

    def kernel(at_ref, rot_ref, own_ref, other_ref, attn_ref, probs_ref):
        even = at_ref[CORE] == 0
        key = jnp.where(even, own_ref[...], other_ref[...])
        value = jnp.where(even, other_ref[...], own_ref[...])
        row = lax.broadcasted_iota(jnp.int32, (length, length), 0)
        column = lax.broadcasted_iota(jnp.int32, (length, length), 1)
        for h in range(heads):
            place = slice(h * head, (h + 1) * head)
            scores = jnp.where(row >= column, nt(rot_ref[:, place], key) * scale, -1e30)
            expo = jnp.exp(scores - jnp.max(scores, axis=-1, keepdims=True))
            probs = expo / jnp.sum(expo, axis=-1, keepdims=True)
            probs_ref[h] = probs
            attn_ref[:, place] = nn(probs.astype(bf16), value).astype(bf16)

    return call(
        kernel,
        "attend",
        order,
        [whole(rot), whole(own), whole(other)],
        [
            whole_out((length, q_width)),
            whole_out((heads, length, length), f32),
        ],
    )


def split_rows(at_ref, product, rows_ref, send_ref, keep_ref):
    rows_ref[...] = product.reshape(rows_ref.shape)
    send_ref[...] = rows_ref[:, 1 - at_ref[CORE]].astype(bf16)
    keep_ref[...] = rows_ref[:, at_ref[CORE]].astype(bf16)


def mix(order, attn, o_weight):
    length, q_width = attn.shape
    full = o_weight.shape[1]
    tile = 1024

    def kernel(at_ref, attn_ref, w_ref, send_ref, keep_ref, rows_ref):
        split_rows(at_ref, nn(attn_ref[...], w_ref[...]), rows_ref, send_ref, keep_ref)

    out = (shape((length // 32, 16, full)), pl.BlockSpec((length // 32, 16, tile), lambda i, at: (0, 0, i)))
    return call(
        kernel,
        "mix",
        order,
        [whole(attn), (o_weight, pl.BlockSpec((q_width, tile), lambda i, at: (0, i)))],
        [out, out],
        grid=(full // tile,),
        scratch=[pltpu.VMEM((length // 32, 2, 16, tile), f32)],
    )


def pair_sum(order, keep, arrived, groups, index):
    chips, _, full = keep.shape
    each = chips // groups
    tile = 2048

    def kernel(at_ref, keep_ref, arrived_ref, *out):
        for k in range(groups):
            here = pl.ds((at_ref[index] ^ k) * each, each) if groups > 1 else slice(None)
            out[k][...] = (keep_ref[here].astype(f32) + arrived_ref[here].astype(f32)).astype(bf16)

    block = pl.BlockSpec((chips, 16, tile), lambda i, at: (0, 0, i))
    out = (shape((each, 16, full)), pl.BlockSpec((each, 16, tile), lambda i, at: (0, 0, i)))
    return call(
        kernel,
        "pair_sum",
        order,
        [(keep, block), (arrived, block)],
        [out] * groups,
        grid=(full // tile,),
    )


def ring_sum(order, parts):
    _, _, full = parts[0].shape
    tile = 2048

    def kernel(at_ref, *refs):
        parts, keep_ref, send_ref = refs[:4], refs[4], refs[5]
        for target, x in ((keep_ref, at_ref[X]), (send_ref, 1 - at_ref[X])):
            total = parts[0][x].astype(f32)
            for part in parts[1:]:
                total += part[x].astype(f32)
            target[...] = total.astype(target.dtype)

    block = pl.BlockSpec((2, 16, tile), lambda i, at: (0, 0, i))
    out = pl.BlockSpec((16, tile), lambda i, at: (0, i))
    return call(
        kernel,
        "ring_sum",
        order,
        [(part, block) for part in parts],
        [(shape((16, full), f32), out), (shape((16, full)), out)],
        grid=(full // tile,),
    )


def out_gradient(order, own, other, o_weight):
    chips, length, width = own.shape
    q_width, full = o_weight.shape

    def kernel(at_ref, own_ref, other_ref, w_ref, dattn_ref, rows_ref, acc):
        step = pl.program_id(0)
        core = at_ref[CORE]

        @pl.when(step == 0)
        def _():
            acc[...] = jnp.zeros_like(acc)

        mine = pl.ds(pl.multiple_of(at_ref[T] * 16, 16), 16)
        for ref, half in ((own_ref, core), (other_ref, 1 - core)):
            place = pl.ds(pl.multiple_of(half * width, width), width)
            acc[...] += nt(ref[0], w_ref[:, place])
            rows_ref[:, place] = ref[0, mine, :]

        @pl.when(step == pl.num_programs(0) - 1)
        def _():
            dattn_ref[...] = acc[...].astype(bf16)

    block = pl.BlockSpec((1, length, width), lambda i, at: (i, 0, 0))
    return call(
        kernel,
        "out_gradient",
        order,
        [
            (own, block),
            (other, block),
            (o_weight, pl.BlockSpec((q_width, 2 * width), lambda i, at: (0, at[CHIP] ^ i))),
        ],
        [
            whole_out((length, q_width)),
            (shape((16, full)), pl.BlockSpec((16, 2 * width), lambda i, at: (0, at[CHIP] ^ i))),
        ],
        grid=(chips,),
        scratch=[pltpu.VMEM((length, q_width), f32)],
    )


def attend_gradient(order, dattn, probs, rot, own, other, tables):
    length, q_width = rot.shape
    head = own.shape[1]
    scale = head ** (-0.5)

    def kernel(
        at_ref, dattn_ref, probs_ref, rot_ref, own_ref, other_ref, cos_ref, sin_ref,
        dq_ref, keep_ref, send_ref,
    ):
        even = at_ref[CORE] == 0
        key = jnp.where(even, own_ref[...], other_ref[...])
        value = jnp.where(even, other_ref[...], own_ref[...])
        dkey = jnp.zeros((length, head), f32)
        dvalue = jnp.zeros((length, head), f32)
        for h in range(q_width // head):
            place = slice(h * head, (h + 1) * head)
            probs = probs_ref[h]
            dattn = dattn_ref[:, place]
            dprobs = nt(dattn, value)
            delta = jnp.sum(dprobs * probs, axis=-1, keepdims=True)
            dscores = (probs * (dprobs - delta) * scale).astype(bf16)
            dq_ref[:, place] = turned(nn(dscores, key), cos_ref, sin_ref, -1.0).astype(bf16)
            dkey += tn(dscores, rot_ref[:, place])
            dvalue += tn(probs.astype(bf16), dattn)
        keep_ref[...] = jnp.where(even, dkey, dvalue)
        send_ref[...] = jnp.where(even, dvalue, dkey).astype(bf16)

    return call(
        kernel,
        "attend_gradient",
        order,
        [whole(a) for a in (dattn, probs, rot, own, other, *tables)],
        [whole_out((length, q_width)), whole_out((length, head), f32), whole_out((length, head))],
    )


def join_gradient(order, dq, keep, arrived, inverse, tables):
    length, q_width = dq.shape
    head = keep.shape[1]

    def kernel(
        at_ref, dq_ref, keep_ref, arrived_ref, inverse_ref, cos_ref, sin_ref, out_ref, scaled_ref
    ):
        inverse = inverse_ref[...]
        dq = dq_ref[...]
        out_ref[:, :q_width] = dq
        scaled_ref[:, :q_width] = (dq.astype(f32) * inverse).astype(bf16)
        plain = keep_ref[...] + arrived_ref[...].astype(f32)
        back = turned(plain, cos_ref, sin_ref, -1.0)
        own = jnp.where(at_ref[CORE] == 0, back, plain).astype(bf16)
        out_ref[:, q_width:] = own
        scaled_ref[:, q_width:] = (own.astype(f32) * inverse).astype(bf16)

    return call(
        kernel,
        "join_gradient",
        order,
        [whole(a) for a in (dq, keep, arrived, inverse, *tables)],
        [whole_out((length, q_width + head))] * 2,
    )


def norm_gradient(order, dqkv, q_weight, kv_weight, normed, gain_row):
    length, full = normed.shape
    q_width, head = q_weight.shape[1], kv_weight.shape[1]
    tile = 1024

    def kernel(
        at_ref, d_ref, q_ref, kv_ref, normed_ref, gain_ref, send_ref, keep_ref, part_ref, rows_ref
    ):
        product = nt(d_ref[:, :q_width], q_ref[...]) + nt(d_ref[:, q_width:], kv_ref[...])
        part = jnp.sum(product * normed_ref[...].astype(f32), axis=0, keepdims=True)
        part_ref[0] = part / gain_ref[...]
        split_rows(at_ref, product, rows_ref, send_ref, keep_ref)

    out = (shape((length // 32, 16, full)), pl.BlockSpec((length // 32, 16, tile), lambda i, at: (0, 0, i)))
    return call(
        kernel,
        "norm_gradient",
        order,
        [
            whole(dqkv),
            (q_weight, pl.BlockSpec((tile, q_width), lambda i, at: (i, 0))),
            (kv_weight, pl.BlockSpec((tile, head), lambda i, at: (i, 0))),
            (normed, pl.BlockSpec((length, tile), lambda i, at: (0, i))),
            (gain_row, pl.BlockSpec((1, tile), lambda i, at: (0, i))),
        ],
        [out, out, (shape((full // tile, 1, tile), f32), pl.BlockSpec((1, 1, tile), lambda i, at: (i, 0, 0)))],
        grid=(full // tile,),
        scratch=[pltpu.VMEM((length // 32, 2, 16, tile), f32)],
    )


def input_gradient(order, keep, arrived, tokens, inverse, cotangent, gain_row):
    rows, full = tokens.shape

    def kernel(
        at_ref, keep_ref, arrived_ref, tokens_ref, inverse_ref, cot_ref, gain_ref, out_ref,
        xhat_ref, scaled_ref,
    ):
        inverse = inverse_ref[pl.ds(pl.multiple_of(at_ref[T] * 16, 16), 16), :]
        tile = 1024
        dots = jnp.zeros((rows, tile), f32)
        for i in range(full // tile):
            place = slice(i * tile, (i + 1) * tile)
            total = keep_ref[:, place] + arrived_ref[:, place].astype(f32)
            xhat = tokens_ref[:, place].astype(f32) * inverse
            scaled = total * gain_ref[:, place]
            xhat_ref[:, place] = xhat
            scaled_ref[:, place] = scaled
            dots += scaled * xhat
        mean = jnp.sum(dots, axis=-1, keepdims=True) / full
        for i in range(full // tile):
            place = slice(i * tile, (i + 1) * tile)
            change = inverse * (scaled_ref[:, place] - xhat_ref[:, place] * mean)
            out_ref[:, place] = (cot_ref[:, place].astype(f32) + change).astype(bf16)

    return call(
        kernel,
        "input_gradient",
        order,
        [whole(a) for a in (keep, arrived, tokens, inverse, cotangent, gain_row)],
        [whole_out((rows, full))],
        scratch=[pltpu.VMEM((rows, full), f32)] * 2,
    )[0]


def out_terms(name, order, own, other, rows, keep, *passed):
    _, length, width = own.shape
    total = rows.shape[2]
    count = len(passed)

    def kernel(at_ref, own_ref, other_ref, rows_ref, *refs):
        sources, out_ref, copies, turned_ref = refs[:count], refs[count], refs[count + 1 : -1], refs[-1]
        step = pl.program_id(0)

        @pl.when(step == 0)
        def _():
            for source, target in zip(sources, copies):
                target[...] = source[...]
            for k in range(4):
                turned_ref[:, k * length : (k + 1) * length] = rows_ref[k].T

        def put(ref):
            product = nn(turned_ref[...], ref[...].reshape(4 * length, width))
            out_ref[...] = product.astype(out_ref.dtype)

        pl.when(step == 0)(lambda: put(own_ref))
        pl.when(step == 1)(lambda: put(other_ref))

    def side(half, at):
        return jnp.where(half == 0, at[CORE], 1 - at[CORE])

    x_of = (lambda at: at[XL]) if keep else (lambda at: 1 - at[XL])
    block = pl.BlockSpec((4, 1, length, width), lambda i, at: (0, x_of(at), 0, 0))
    dims = (4, 2, length, width)
    return call(
        kernel,
        name,
        order,
        [(own.reshape(dims), block), (other.reshape(dims), block), whole(rows)]
        + [whole(p) for p in passed],
        [
            (
                shape((total, 2 * width), f32 if keep else bf16),
                pl.BlockSpec((total, width), lambda i, at: (0, side(i, at))),
            )
        ]
        + [whole_out(p.shape, p.dtype) for p in passed],
        grid=(2,),
        scratch=[pltpu.VMEM((total, 4 * length), bf16)],
    )


def add_terms(order, keep, arrived):
    rows, columns = keep.shape
    block = pl.BlockSpec((rows // 4, columns), lambda i, at: (i, 0))

    def kernel(at_ref, keep_ref, arrived_ref, out_ref):
        out_ref[...] = keep_ref[...] + arrived_ref[...].astype(f32)

    return call(
        kernel,
        "add_terms",
        order,
        [(keep, block), (arrived, block)],
        [(shape((rows, columns), f32), block)],
        grid=(4,),
    )[0]


def q_gradient(order, own, other, rows, gain_column, q_width):
    _, width, wide = own.shape
    length, total = rows[0].shape[1:]
    head = total - q_width

    def kernel(at_ref, *refs):
        own_ref, other_ref, row_refs, gain_ref = *refs[:2], refs[2:6], refs[6]
        q_out, kv_out, acc, joined = refs[7:]
        half = pl.program_id(0)

        @pl.when(half == 0)
        def _():
            for k in range(4):
                for x in range(2):
                    joined[x, k * length : (k + 1) * length, :] = row_refs[k][x]

        def add(ref):
            acc[...] = nn(ref[0], joined[0])
            acc[...] += nn(ref[1], joined[1])

        pl.when(half == 0)(lambda: add(own_ref))
        pl.when(half == 1)(lambda: add(other_ref))
        q_out[...] = acc[:, :q_width] * gain_ref[...]
        kv_out[...] = acc[:, q_width:] * gain_ref[...]

    def side(h, at):
        return jnp.where(h == 0, at[CORE], 1 - at[CORE])

    return call(
        kernel,
        "q_gradient",
        order,
        [whole(own), whole(other)]
        + [whole(a) for a in rows]
        + [
            (gain_column, pl.BlockSpec((width, 1), lambda h, at: (side(h, at), 0))),
        ],
        [
            (
                shape((2 * width, size), f32),
                pl.BlockSpec((width, size), lambda h, at: (side(h, at), 0)),
            )
            for size in (q_width, head)
        ],
        grid=(2,),
        scratch=[pltpu.VMEM((width, total), f32), pltpu.VMEM((2, 4 * length, total), bf16)],
    )


def near(parts):
    return {k: partner(parts[k], "dp", 2 * k) for k in (1, 3)}


def far(parts):
    return {2: partner(parts[2], "dp", 4)}


def in_order(*found):
    merged = {}
    for part in found:
        merged.update(part)
    return [merged[k] for k in sorted(merged)]


def split_x(name, order, parts):
    _, width, length = parts[0].shape

    def plan(at_ref, ins, outs):
        pairs = []
        for k, ref in enumerate(ins):
            place = pl.ds(k * length, length)
            pairs.append((ref.at[at_ref[XL]], outs[0].at[:, place]))
            pairs.append((ref.at[1 - at_ref[XL]], outs[1].at[:, place]))
        return pairs

    return move(name, order, parts, [shape((width, len(parts) * length))] * 2, plan)


def stack_b(order, parts):
    _, length, width = parts[0].shape

    def plan(at_ref, ins, outs):
        pairs = [(ref.at[pl.ds(0, 2)], outs[0].at[pl.ds(2 * k, 2)]) for k, ref in enumerate(ins)]
        return pairs + [(ref.at[2], outs[1].at[k]) for k, ref in enumerate(ins)]

    return move(
        "stack_b", order, parts, [shape((8, length, width)), shape((4, length, width))], plan
    )


def rotary(length, head):
    freq = theta ** (-(np.arange(head // 2, dtype=np.float64) * 2.0 / head))
    angle = np.arange(length, dtype=np.float64)[:, None] * freq[None, :]
    cosine, sine = np.cos(angle), np.sin(angle)
    return (
        np.concatenate([cosine, cosine], 1).astype(np.float32),
        np.concatenate([-sine, sine], 1).astype(np.float32),
    )


def on_device(tokens, gain, q_weight, kv_weight, o_weight, out_grad):
    t_at = lax.axis_index("tensor")
    dp_at = lax.axis_index("dp")
    at = jnp.stack(
        [t_at, t_at // 2, t_at % 2, t_at // 4, t_at // 2 % 2, dp_at // 2, dp_at % 2]
    ).astype(jnp.int32)
    order = Order(at)
    length, width = tokens.shape[1:]
    q_width, head = q_weight.shape[1], kv_weight.shape[1]
    tables = [jnp.asarray(table) for table in rotary(length, head)]
    gain_float = gain.astype(f32)
    gain_row = gain_float[None, :]
    gain_column = lax.dynamic_slice_in_dim(gain_float, dp_at * 2 * width, 2 * width)[:, None]

    def y_near(parts):
        return {k: partner(parts[k], "tensor", 4 * k) for k in (1, 3)}

    def y_far(parts):
        return {2: partner(parts[2], "tensor", 8)}

    shard, cot = tokens[0], out_grad[0]
    shards = {0: shard, 1: partner(shard, "tensor", 2)}
    for j in (2, 6, 4):
        shards[j] = partner(shard, "tensor", 2 * j)
    for j in (2, 6, 4):
        shards[j ^ 1] = partner(shards[1], "tensor", 2 * j)
    cot_other = partner(cot, "tensor", 2)
    own, cot_pair = stack("stack_tokens", order, [shards[j] for j in range(8)], [cot, cot_other])
    other = partner(own, "tensor", 1)
    cot_near = y_near([cot_pair] * 4)

    blocks = dict(zip((0, 1, 3), pick_tokens("pick_near", order, own, (0, 1, 3))))
    token_near = near(blocks)
    normed, inverse, own_tokens = norm(order, gain_row, own, other)
    rot, kv_own = project(order, normed, q_weight, kv_weight, tables)
    blocks[2], cot_copy = pick_tokens("pick_far", order, own, (2,), cot_pair)
    cot_far = y_far([cot_copy] * 4)
    kv_other = partner(kv_own, "tensor", 1)
    token_far = far(blocks)
    order.wait(*token_near.values(), *cot_near.values())
    attn, probs = attend(order, rot, kv_own, kv_other)
    send, keep = mix(order, attn, o_weight)
    arrived = partner(send, "tensor", 1)

    order.wait(*token_far.values())
    (cot_own,) = stack("stack_cot", order, in_order({0: cot_pair}, cot_near, cot_far))
    cot_other = partner(cot_own, "tensor", 1)

    def cot_plan(at_ref, ins, outs):
        return [
            (ins[0].at[at_ref[CHIP] ^ (2 * (at_ref[Z] ^ k) + x)], outs[k].at[x])
            for k in range(4)
            for x in range(2)
        ] + [(ins[1], outs[k].at[2]) for k in range(4)]

    cot_blocks = move(
        "pick_cot", order, [cot_own, attn], [shape((3, length, width))] * 4, cot_plan
    )
    b_near = near(cot_blocks)
    a_keep, a_send = split_x(
        "split_tokens", order, in_order({0: blocks[0]}, token_near, token_far)
    )
    a_cross = partner(a_send, "dp", 1)
    out_parts = pair_sum(order, keep, arrived, 4, Y)
    out_near = y_near(out_parts)
    dattn, own_cot = out_gradient(order, cot_own, cot_other, o_weight)
    dq, dkv_keep, send = attend_gradient(order, dattn, probs, rot, kv_own, kv_other, tables)
    arrived = partner(send, "tensor", 1)
    order.wait(*b_near.values(), *out_near.values(), a_cross)
    dqkv, scaled = join_gradient(order, dq, dkv_keep, arrived, inverse, tables)
    scaled_other = partner(scaled, "dp", 1)
    b_far = far(cot_blocks)
    out_far = y_far(out_parts)
    send, keep, gain_part = norm_gradient(order, dqkv, q_weight, kv_weight, normed, gain_row)
    arrived = partner(send, "tensor", 1)
    x_parts = pair_sum(order, keep, arrived, 4, Y)
    x_near = y_near(x_parts)
    gain_part = jnp.sum(lax.all_to_all(gain_part, "dp", 0, 0, tiled=True), axis=0)
    gain_part = lax.all_to_all(
        jnp.broadcast_to(gain_part[None], (16, 1, 2 * width)), "tensor", 0, 0, tiled=True
    )
    gain_grad = jnp.sum(gain_part, axis=0)
    order.wait(*b_far.values(), *out_far.values(), *x_near.values(), gain_grad)
    pair, a_own = stack("stack_dqkv", order, [scaled, scaled_other], [a_keep, a_cross])
    dqkv_near = near([pair] * 4)
    b_own, attn_all = stack_b(order, in_order({0: cot_blocks[0]}, b_near, b_far))
    b_other = partner(b_own, "tensor", 1)
    x_far = y_far(x_parts)
    (keep,) = out_terms("out_keep", order, b_own, b_other, attn_all, True)
    out_keep, out_send = ring_sum(order, in_order({0: out_parts[0]}, out_near, out_far))
    out_arrived = partner(out_send, "tensor", 2)
    x_keep, x_send = ring_sum(order, in_order({0: x_parts[0]}, x_near, x_far))
    x_arrived = partner(x_send, "tensor", 2)
    order.wait(*dqkv_near.values())
    send, pair_copy = out_terms("out_send", order, b_own, b_other, attn_all, False, pair)
    o_arrived = partner(send, "dp", 1)
    dqkv_far = far([pair_copy] * 4)
    a_other = partner(a_own, "tensor", 1)
    result = (own_tokens.astype(f32) + (out_keep + out_arrived.astype(f32))).astype(bf16)
    order.vmem = LATE
    q_grad, kv_grad = q_gradient(
        order,
        a_own,
        a_other,
        in_order({0: pair}, dqkv_near, dqkv_far),
        gain_column,
        q_width,
    )
    order.vmem = VMEM
    order.wait(o_arrived)
    x_grad = input_gradient(order, x_keep, x_arrived, own_tokens, inverse, own_cot, gain_row)
    o_grad = add_terms(order, keep, o_arrived)
    return (result[None], x_grad[None], gain_grad.reshape(-1), q_grad, kv_grad, o_grad)


def solution(mesh):
    in_specs = (
        P("dp", None, "tensor"),
        P(),
        P(None, "tensor"),
        P(None, "tensor"),
        P("tensor", None),
        P("dp", None, "tensor"),
    )
    out_specs = (
        P("dp", "tensor", None),
        P("dp", "tensor", None),
        P("dp"),
        P("dp", "tensor"),
        P("dp", "tensor"),
        P("tensor", "dp"),
    )
    return jax.shard_map(
        on_device, mesh=mesh, in_specs=in_specs, out_specs=out_specs, check_vma=False
    )
```

```python
import jax
import jax.numpy as jnp
import numpy as np
from jax import lax
from jax.experimental import pallas as pl
from jax.experimental.pallas import tpu as pltpu
from jax.sharding import PartitionSpec as P

epsilon = 1e-05
theta = 500000.0
f32 = jnp.float32
bf16 = jnp.bfloat16
VMEM = 16 * 1024 * 1024
LATE = 58 * 1024 * 1024
ANY = pl.BlockSpec(memory_space=pl.ANY)
T, CHIP, CORE, Y, X, Z, XL = range(7)


def partner(array, axis, bits):
    return lax.ppermute(array, axis, [(i, i ^ bits) for i in range(lax.axis_size(axis))])


class Order:
    def __init__(self, at):
        self.at, self.last, self.vmem = at, [], VMEM

    def wait(self, *arrays):
        self.last = self.last + list(arrays)


def call(kernel, name, order, operands, outputs, grid=(1,), scratch=()):
    arrays = [array for array, _ in operands]
    after = order.last
    count, extra, results = len(arrays), len(after), len(outputs)

    def body(at_ref, *refs):
        outs = refs[count + extra :]
        outs[results][...] = jnp.zeros_like(outs[results])
        kernel(at_ref, *refs[:count], *outs[:results], *outs[results + 1 :])

    outputs = outputs + [whole_out((8, 128), f32)]

    results = pl.pallas_call(
        body,
        grid_spec=pltpu.PrefetchScalarGridSpec(
            num_scalar_prefetch=1,
            grid=grid,
            in_specs=[spec for _, spec in operands] + [ANY] * extra,
            out_specs=[spec for _, spec in outputs],
            scratch_shapes=list(scratch),
        ),
        out_shape=[shape for shape, _ in outputs],
        compiler_params=pltpu.CompilerParams(vmem_limit_bytes=order.vmem),
        cost_estimate=pl.CostEstimate(flops=1, bytes_accessed=1, transcendentals=0),
        name=name,
    )(order.at, *arrays, *after)
    results = list(results)
    order.last = [results.pop()]
    return results


def whole(array):
    rank = len(array.shape)
    return (array, pl.BlockSpec(tuple(array.shape), lambda *_: (0,) * rank))


def shape(dims, dtype=bf16):
    return jax.ShapeDtypeStruct(tuple(dims), dtype)


def nt(left, right):
    return lax.dot_general(left, right, (((1,), (1,)), ((), ())), preferred_element_type=f32)


def tn(left, right):
    return lax.dot_general(left, right, (((0,), (0,)), ((), ())), preferred_element_type=f32)


def nn(left, right):
    return jnp.dot(left, right, preferred_element_type=f32)


def move(name, order, sources, out_shapes, plan):
    count, outs_count = len(sources), len(out_shapes)

    def kernel(at_ref, *refs):
        ins, outs = refs[:count], refs[count : count + outs_count]
        held, sems, out_sems = refs[count + outs_count : -2], refs[-2], refs[-1]
        copies = [
            pltpu.make_async_copy(source, target, sems.at[number])
            for number, (source, target) in enumerate(plan(at_ref, ins, held))
        ]
        for copy in copies:
            copy.start()
        for copy in copies:
            copy.wait()
        copies = [
            pltpu.make_async_copy(source, target, out_sems.at[number])
            for number, (source, target) in enumerate(zip(held, outs))
        ]
        for copy in copies:
            copy.start()
        for copy in copies:
            copy.wait()

    return call(
        kernel,
        name,
        order,
        [(source, ANY) for source in sources],
        [(s, ANY) for s in out_shapes],
        scratch=[pltpu.VMEM(s.shape, s.dtype) for s in out_shapes]
        + [pltpu.SemaphoreType.DMA((16,))] * 2,
    )


def stack(name, order, *groups):
    groups = [[p if p.ndim == 3 else p[None] for p in group] for group in groups]
    sources = [p for group in groups for p in group]

    def plan(at_ref, ins, outs):
        pairs, number = [], 0
        for group, out in zip(groups, outs):
            row = 0
            for p in group:
                pairs.append((ins[number], out.at[pl.ds(row, p.shape[0])]))
                row += p.shape[0]
                number += 1
        return pairs

    outs = [shape((sum(p.shape[0] for p in g),) + g[0].shape[1:], g[0].dtype) for g in groups]
    return move(name, order, sources, outs, plan)


def norm(order, gain_row, own, other):
    chips, length, width = own.shape
    tile = 64
    full = 2 * chips * width

    def kernel(at_ref, gain_ref, own_ref, other_ref, normed_ref, inverse_ref, rows_ref):
        chip, core = at_ref[CHIP], at_ref[CORE]

        def columns(pair, half):
            return pl.ds(pl.multiple_of((2 * pair + half) * width, width), width)

        @pl.loop(0, tile // 16)
        def _(step):
            here = pl.ds(pl.multiple_of(step * 16, 16), 16)
            squares = jnp.zeros((16, width), f32)
            for j in range(chips):
                for ref in (own_ref, other_ref):
                    value = ref[j, here, :].astype(f32)
                    squares += value * value
            mean = jnp.sum(squares, axis=-1, keepdims=True) / full
            inverse = lax.rsqrt(mean + epsilon)
            inverse_ref[here, :] = inverse
            for j in range(chips):
                for ref, half in ((own_ref, core), (other_ref, 1 - core)):
                    place = columns(chip ^ j, half)
                    value = ref[j, here, :].astype(f32)
                    normed_ref[here, place] = (value * inverse * gain_ref[:, place]).astype(bf16)

            @pl.when(pl.program_id(0) * (tile // 16) + step == at_ref[T])
            def _():
                for j in range(chips):
                    for ref, half in ((own_ref, core), (other_ref, 1 - core)):
                        rows_ref[:, columns(chip ^ j, half)] = ref[j, here, :]

    block = pl.BlockSpec((chips, tile, width), lambda i, at: (0, i, 0))
    return call(
        kernel,
        "norm",
        order,
        [whole(gain_row), (own, block), (other, block)],
        [
            (shape((length, full)), pl.BlockSpec((tile, full), lambda i, at: (i, 0))),
            (shape((length, 1), f32), pl.BlockSpec((tile, 1), lambda i, at: (i, 0))),
            (shape((16, full)), pl.BlockSpec((16, full), lambda i, at: (0, 0))),
        ],
        grid=(length // tile,),
    )


def pick_tokens(name, order, own, partners, *copied):
    chips, length, width = own.shape
    count = len(partners)

    def kernel(at_ref, own_ref, *refs):
        ins, out, copies = refs[: len(copied)], refs[len(copied) :][:count], refs[len(copied) + count :]
        for number, k in enumerate(partners):
            for x in range(2):
                out[number][x] = own_ref[at_ref[CHIP] ^ (2 * (at_ref[Z] ^ k) + x)].T
        for source, target in zip(ins, copies):
            target[...] = source[...]

    return call(
        kernel,
        name,
        order,
        [whole(own)] + [whole(c) for c in copied],
        [whole_out((2, width, length))] * count + [whole_out(c.shape) for c in copied],
    )


def turned(value, cos_ref, sin_ref, direction):
    swapped = pltpu.roll(value, value.shape[-1] // 2, 1)
    return value * cos_ref[...] + swapped * (sin_ref[...] * direction)


def project(order, normed, q_weight, kv_weight, tables):
    length, full = normed.shape
    q_width, head = q_weight.shape[1], kv_weight.shape[1]
    tile = 1024

    def kernel(at_ref, x_ref, q_ref, kv_ref, cos_ref, sin_ref, rot_ref, own_ref, qacc, kvacc):
        step = pl.program_id(0)

        @pl.when(step == 0)
        def _():
            qacc[...] = jnp.zeros_like(qacc)
            kvacc[...] = jnp.zeros_like(kvacc)

        qacc[...] += nn(x_ref[...], q_ref[...])
        kvacc[...] += nn(x_ref[...], kv_ref[...])

        @pl.when(step == pl.num_programs(0) - 1)
        def _():
            for h in range(q_width // head):
                place = slice(h * head, (h + 1) * head)
                rot_ref[:, place] = turned(qacc[:, place], cos_ref, sin_ref, 1.0).astype(bf16)
            plain = kvacc[...]
            rotated = turned(plain, cos_ref, sin_ref, 1.0)
            own_ref[...] = jnp.where(at_ref[CORE] == 0, rotated, plain).astype(bf16)

    return call(
        kernel,
        "project",
        order,
        [
            (normed, pl.BlockSpec((length, tile), lambda i, at: (0, i))),
            (q_weight, pl.BlockSpec((tile, q_width), lambda i, at: (i, 0))),
            (kv_weight, pl.BlockSpec((tile, head), lambda i, at: (i, 0))),
            whole(tables[0]),
            whole(tables[1]),
        ],
        [whole_out((length, q_width)), whole_out((length, head))],
        grid=(full // tile,),
        scratch=[pltpu.VMEM((length, q_width), f32), pltpu.VMEM((length, head), f32)],
    )


def whole_out(dims, dtype=bf16):
    return whole(shape(dims, dtype))


def attend(order, rot, own, other):
    length, q_width = rot.shape
    head = own.shape[1]
    heads = q_width // head
    scale = head ** (-0.5)

    def kernel(at_ref, rot_ref, own_ref, other_ref, attn_ref, probs_ref):
        even = at_ref[CORE] == 0
        key = jnp.where(even, own_ref[...], other_ref[...])
        value = jnp.where(even, other_ref[...], own_ref[...])
        row = lax.broadcasted_iota(jnp.int32, (length, length), 0)
        column = lax.broadcasted_iota(jnp.int32, (length, length), 1)
        for h in range(heads):
            place = slice(h * head, (h + 1) * head)
            scores = jnp.where(row >= column, nt(rot_ref[:, place], key) * scale, -1e30)
            expo = jnp.exp(scores - jnp.max(scores, axis=-1, keepdims=True))
            probs = expo / jnp.sum(expo, axis=-1, keepdims=True)
            probs_ref[h] = probs
            attn_ref[:, place] = nn(probs.astype(bf16), value).astype(bf16)

    return call(
        kernel,
        "attend",
        order,
        [whole(rot), whole(own), whole(other)],
        [
            whole_out((length, q_width)),
            whole_out((heads, length, length), f32),
        ],
    )


def split_rows(at_ref, product, rows_ref, send_ref, keep_ref):
    rows_ref[...] = product.reshape(rows_ref.shape)
    send_ref[...] = rows_ref[:, 1 - at_ref[CORE]].astype(bf16)
    keep_ref[...] = rows_ref[:, at_ref[CORE]].astype(bf16)


def mix(order, attn, o_weight):
    length, q_width = attn.shape
    full = o_weight.shape[1]
    tile = 1024

    def kernel(at_ref, attn_ref, w_ref, send_ref, keep_ref, rows_ref):
        split_rows(at_ref, nn(attn_ref[...], w_ref[...]), rows_ref, send_ref, keep_ref)

    out = (shape((length // 32, 16, full)), pl.BlockSpec((length // 32, 16, tile), lambda i, at: (0, 0, i)))
    return call(
        kernel,
        "mix",
        order,
        [whole(attn), (o_weight, pl.BlockSpec((q_width, tile), lambda i, at: (0, i)))],
        [out, out],
        grid=(full // tile,),
        scratch=[pltpu.VMEM((length // 32, 2, 16, tile), f32)],
    )


def pair_sum(order, keep, arrived, groups, index):
    chips, _, full = keep.shape
    each = chips // groups
    tile = 2048

    def kernel(at_ref, keep_ref, arrived_ref, *out):
        for k in range(groups):
            here = pl.ds((at_ref[index] ^ k) * each, each) if groups > 1 else slice(None)
            out[k][...] = (keep_ref[here].astype(f32) + arrived_ref[here].astype(f32)).astype(bf16)

    block = pl.BlockSpec((chips, 16, tile), lambda i, at: (0, 0, i))
    out = (shape((each, 16, full)), pl.BlockSpec((each, 16, tile), lambda i, at: (0, 0, i)))
    return call(
        kernel,
        "pair_sum",
        order,
        [(keep, block), (arrived, block)],
        [out] * groups,
        grid=(full // tile,),
    )


def ring_sum(order, parts):
    _, _, full = parts[0].shape
    tile = 2048

    def kernel(at_ref, *refs):
        parts, keep_ref, send_ref = refs[:4], refs[4], refs[5]
        for target, x in ((keep_ref, at_ref[X]), (send_ref, 1 - at_ref[X])):
            total = parts[0][x].astype(f32)
            for part in parts[1:]:
                total += part[x].astype(f32)
            target[...] = total.astype(target.dtype)

    block = pl.BlockSpec((2, 16, tile), lambda i, at: (0, 0, i))
    out = pl.BlockSpec((16, tile), lambda i, at: (0, i))
    return call(
        kernel,
        "ring_sum",
        order,
        [(part, block) for part in parts],
        [(shape((16, full), f32), out), (shape((16, full)), out)],
        grid=(full // tile,),
    )


def out_gradient(order, own, other, o_weight):
    chips, length, width = own.shape
    q_width, full = o_weight.shape

    def kernel(at_ref, own_ref, other_ref, w_ref, dattn_ref, rows_ref, acc):
        step = pl.program_id(0)
        core = at_ref[CORE]

        @pl.when(step == 0)
        def _():
            acc[...] = jnp.zeros_like(acc)

        mine = pl.ds(pl.multiple_of(at_ref[T] * 16, 16), 16)
        for ref, half in ((own_ref, core), (other_ref, 1 - core)):
            place = pl.ds(pl.multiple_of(half * width, width), width)
            acc[...] += nt(ref[0], w_ref[:, place])
            rows_ref[:, place] = ref[0, mine, :]

        @pl.when(step == pl.num_programs(0) - 1)
        def _():
            dattn_ref[...] = acc[...].astype(bf16)

    block = pl.BlockSpec((1, length, width), lambda i, at: (i, 0, 0))
    return call(
        kernel,
        "out_gradient",
        order,
        [
            (own, block),
            (other, block),
            (o_weight, pl.BlockSpec((q_width, 2 * width), lambda i, at: (0, at[CHIP] ^ i))),
        ],
        [
            whole_out((length, q_width)),
            (shape((16, full)), pl.BlockSpec((16, 2 * width), lambda i, at: (0, at[CHIP] ^ i))),
        ],
        grid=(chips,),
        scratch=[pltpu.VMEM((length, q_width), f32)],
    )


def attend_gradient(order, dattn, probs, rot, own, other, tables):
    length, q_width = rot.shape
    head = own.shape[1]
    scale = head ** (-0.5)

    def kernel(
        at_ref, dattn_ref, probs_ref, rot_ref, own_ref, other_ref, cos_ref, sin_ref,
        dq_ref, keep_ref, send_ref,
    ):
        even = at_ref[CORE] == 0
        key = jnp.where(even, own_ref[...], other_ref[...])
        value = jnp.where(even, other_ref[...], own_ref[...])
        dkey = jnp.zeros((length, head), f32)
        dvalue = jnp.zeros((length, head), f32)
        for h in range(q_width // head):
            place = slice(h * head, (h + 1) * head)
            probs = probs_ref[h]
            dattn = dattn_ref[:, place]
            dprobs = nt(dattn, value)
            delta = jnp.sum(dprobs * probs, axis=-1, keepdims=True)
            dscores = (probs * (dprobs - delta) * scale).astype(bf16)
            dq_ref[:, place] = turned(nn(dscores, key), cos_ref, sin_ref, -1.0).astype(bf16)
            dkey += tn(dscores, rot_ref[:, place])
            dvalue += tn(probs.astype(bf16), dattn)
        keep_ref[...] = jnp.where(even, dkey, dvalue)
        send_ref[...] = jnp.where(even, dvalue, dkey).astype(bf16)

    return call(
        kernel,
        "attend_gradient",
        order,
        [whole(a) for a in (dattn, probs, rot, own, other, *tables)],
        [whole_out((length, q_width)), whole_out((length, head), f32), whole_out((length, head))],
    )


def join_gradient(order, dq, keep, arrived, inverse, tables):
    length, q_width = dq.shape
    head = keep.shape[1]

    def kernel(
        at_ref, dq_ref, keep_ref, arrived_ref, inverse_ref, cos_ref, sin_ref, out_ref, scaled_ref
    ):
        inverse = inverse_ref[...]
        dq = dq_ref[...]
        out_ref[:, :q_width] = dq
        scaled_ref[:, :q_width] = (dq.astype(f32) * inverse).astype(bf16)
        plain = keep_ref[...] + arrived_ref[...].astype(f32)
        back = turned(plain, cos_ref, sin_ref, -1.0)
        own = jnp.where(at_ref[CORE] == 0, back, plain).astype(bf16)
        out_ref[:, q_width:] = own
        scaled_ref[:, q_width:] = (own.astype(f32) * inverse).astype(bf16)

    return call(
        kernel,
        "join_gradient",
        order,
        [whole(a) for a in (dq, keep, arrived, inverse, *tables)],
        [whole_out((length, q_width + head))] * 2,
    )


def norm_gradient(order, dqkv, q_weight, kv_weight, normed, gain_row):
    length, full = normed.shape
    q_width, head = q_weight.shape[1], kv_weight.shape[1]
    tile = 1024

    def kernel(
        at_ref, d_ref, q_ref, kv_ref, normed_ref, gain_ref, send_ref, keep_ref, part_ref, rows_ref
    ):
        product = nt(d_ref[:, :q_width], q_ref[...]) + nt(d_ref[:, q_width:], kv_ref[...])
        part = jnp.sum(product * normed_ref[...].astype(f32), axis=0, keepdims=True)
        part_ref[0] = part / gain_ref[...]
        split_rows(at_ref, product, rows_ref, send_ref, keep_ref)

    out = (shape((length // 32, 16, full)), pl.BlockSpec((length // 32, 16, tile), lambda i, at: (0, 0, i)))
    return call(
        kernel,
        "norm_gradient",
        order,
        [
            whole(dqkv),
            (q_weight, pl.BlockSpec((tile, q_width), lambda i, at: (i, 0))),
            (kv_weight, pl.BlockSpec((tile, head), lambda i, at: (i, 0))),
            (normed, pl.BlockSpec((length, tile), lambda i, at: (0, i))),
            (gain_row, pl.BlockSpec((1, tile), lambda i, at: (0, i))),
        ],
        [out, out, (shape((full // tile, 1, tile), f32), pl.BlockSpec((1, 1, tile), lambda i, at: (i, 0, 0)))],
        grid=(full // tile,),
        scratch=[pltpu.VMEM((length // 32, 2, 16, tile), f32)],
    )


def input_gradient(order, keep, arrived, tokens, inverse, cotangent, gain_row):
    rows, full = tokens.shape

    def kernel(
        at_ref, keep_ref, arrived_ref, tokens_ref, inverse_ref, cot_ref, gain_ref, out_ref,
        xhat_ref, scaled_ref,
    ):
        inverse = inverse_ref[pl.ds(pl.multiple_of(at_ref[T] * 16, 16), 16), :]
        tile = 1024
        dots = jnp.zeros((rows, tile), f32)
        for i in range(full // tile):
            place = slice(i * tile, (i + 1) * tile)
            total = keep_ref[:, place] + arrived_ref[:, place].astype(f32)
            xhat = tokens_ref[:, place].astype(f32) * inverse
            scaled = total * gain_ref[:, place]
            xhat_ref[:, place] = xhat
            scaled_ref[:, place] = scaled
            dots += scaled * xhat
        mean = jnp.sum(dots, axis=-1, keepdims=True) / full
        for i in range(full // tile):
            place = slice(i * tile, (i + 1) * tile)
            change = inverse * (scaled_ref[:, place] - xhat_ref[:, place] * mean)
            out_ref[:, place] = (cot_ref[:, place].astype(f32) + change).astype(bf16)

    return call(
        kernel,
        "input_gradient",
        order,
        [whole(a) for a in (keep, arrived, tokens, inverse, cotangent, gain_row)],
        [whole_out((rows, full))],
        scratch=[pltpu.VMEM((rows, full), f32)] * 2,
    )[0]


def out_terms(name, order, own, other, rows, keep, *passed):
    _, length, width = own.shape
    total = rows.shape[2]
    count = len(passed)

    def kernel(at_ref, own_ref, other_ref, rows_ref, *refs):
        sources, out_ref, copies, turned_ref = refs[:count], refs[count], refs[count + 1 : -1], refs[-1]
        step = pl.program_id(0)

        @pl.when(step == 0)
        def _():
            for source, target in zip(sources, copies):
                target[...] = source[...]
            for k in range(4):
                turned_ref[:, k * length : (k + 1) * length] = rows_ref[k].T

        def put(ref):
            product = nn(turned_ref[...], ref[...].reshape(4 * length, width))
            out_ref[...] = product.astype(out_ref.dtype)

        pl.when(step == 0)(lambda: put(own_ref))
        pl.when(step == 1)(lambda: put(other_ref))

    def side(half, at):
        return jnp.where(half == 0, at[CORE], 1 - at[CORE])

    x_of = (lambda at: at[XL]) if keep else (lambda at: 1 - at[XL])
    block = pl.BlockSpec((4, 1, length, width), lambda i, at: (0, x_of(at), 0, 0))
    dims = (4, 2, length, width)
    return call(
        kernel,
        name,
        order,
        [(own.reshape(dims), block), (other.reshape(dims), block), whole(rows)]
        + [whole(p) for p in passed],
        [
            (
                shape((total, 2 * width), f32 if keep else bf16),
                pl.BlockSpec((total, width), lambda i, at: (0, side(i, at))),
            )
        ]
        + [whole_out(p.shape, p.dtype) for p in passed],
        grid=(2,),
        scratch=[pltpu.VMEM((total, 4 * length), bf16)],
    )


def add_terms(order, keep, arrived):
    rows, columns = keep.shape
    block = pl.BlockSpec((rows // 4, columns), lambda i, at: (i, 0))

    def kernel(at_ref, keep_ref, arrived_ref, out_ref):
        out_ref[...] = keep_ref[...] + arrived_ref[...].astype(f32)

    return call(
        kernel,
        "add_terms",
        order,
        [(keep, block), (arrived, block)],
        [(shape((rows, columns), f32), block)],
        grid=(4,),
    )[0]


def q_gradient(order, own, other, rows, gain_column, q_width):
    _, width, wide = own.shape
    length, total = rows[0].shape[1:]
    head = total - q_width

    def kernel(at_ref, *refs):
        own_ref, other_ref, row_refs, gain_ref = *refs[:2], refs[2:6], refs[6]
        q_out, kv_out, acc, joined = refs[7:]
        half, x_at = pl.program_id(0), pl.program_id(1)

        @pl.when((half == 0) & (x_at == 0))
        def _():
            for k in range(4):
                for x in range(2):
                    joined[x, k * length : (k + 1) * length, :] = row_refs[k][x]

        def add(ref):
            @pl.when(x_at == 0)
            def _():
                acc[...] = nn(ref[0], joined[0])

            @pl.when(x_at == 1)
            def _():
                total = acc[...] + nn(ref[0], joined[1])
                q_out[...] = total[:, :q_width] * gain_ref[...]
                kv_out[...] = total[:, q_width:] * gain_ref[...]

        pl.when(half == 0)(lambda: add(own_ref))
        pl.when(half == 1)(lambda: add(other_ref))

    def side(h, at):
        return jnp.where(h == 0, at[CORE], 1 - at[CORE])

    return call(
        kernel,
        "q_gradient",
        order,
        [
            (own, pl.BlockSpec((1, width, wide), lambda h, x, at: (jnp.where(h == 0, x, 1), 0, 0))),
            (other, pl.BlockSpec((1, width, wide), lambda h, x, at: (jnp.where(h == 0, 0, x), 0, 0))),
        ]
        + [whole(a) for a in rows]
        + [
            (gain_column, pl.BlockSpec((width, 1), lambda h, x, at: (side(h, at), 0))),
        ],
        [
            (
                shape((2 * width, size), f32),
                pl.BlockSpec((width, size), lambda h, x, at: (side(h, at), 0)),
            )
            for size in (q_width, head)
        ],
        grid=(2, 2),
        scratch=[pltpu.VMEM((width, total), f32), pltpu.VMEM((2, 4 * length, total), bf16)],
    )


def near(parts):
    return {k: partner(parts[k], "dp", 2 * k) for k in (1, 3)}


def far(parts):
    return {2: partner(parts[2], "dp", 4)}


def in_order(*found):
    merged = {}
    for part in found:
        merged.update(part)
    return [merged[k] for k in sorted(merged)]


def split_x(name, order, parts):
    _, width, length = parts[0].shape

    def plan(at_ref, ins, outs):
        pairs = []
        for k, ref in enumerate(ins):
            place = pl.ds(k * length, length)
            pairs.append((ref.at[at_ref[XL]], outs[0].at[:, place]))
            pairs.append((ref.at[1 - at_ref[XL]], outs[1].at[:, place]))
        return pairs

    return move(name, order, parts, [shape((width, len(parts) * length))] * 2, plan)


def stack_b(order, parts):
    _, length, width = parts[0].shape

    def plan(at_ref, ins, outs):
        pairs = [(ref.at[pl.ds(0, 2)], outs[0].at[pl.ds(2 * k, 2)]) for k, ref in enumerate(ins)]
        return pairs + [(ref.at[2], outs[1].at[k]) for k, ref in enumerate(ins)]

    return move(
        "stack_b", order, parts, [shape((8, length, width)), shape((4, length, width))], plan
    )


def rotary(length, head):
    freq = theta ** (-(np.arange(head // 2, dtype=np.float64) * 2.0 / head))
    angle = np.arange(length, dtype=np.float64)[:, None] * freq[None, :]
    cosine, sine = np.cos(angle), np.sin(angle)
    return (
        np.concatenate([cosine, cosine], 1).astype(np.float32),
        np.concatenate([-sine, sine], 1).astype(np.float32),
    )


def on_device(tokens, gain, q_weight, kv_weight, o_weight, out_grad):
    t_at = lax.axis_index("tensor")
    dp_at = lax.axis_index("dp")
    at = jnp.stack(
        [t_at, t_at // 2, t_at % 2, t_at // 4, t_at // 2 % 2, dp_at // 2, dp_at % 2]
    ).astype(jnp.int32)
    order = Order(at)
    length, width = tokens.shape[1:]
    q_width, head = q_weight.shape[1], kv_weight.shape[1]
    tables = [jnp.asarray(table) for table in rotary(length, head)]
    gain_float = gain.astype(f32)
    gain_row = gain_float[None, :]
    gain_column = lax.dynamic_slice_in_dim(gain_float, dp_at * 2 * width, 2 * width)[:, None]

    def y_near(parts):
        return {k: partner(parts[k], "tensor", 4 * k) for k in (1, 3)}

    def y_far(parts):
        return {2: partner(parts[2], "tensor", 8)}

    shard, cot = tokens[0], out_grad[0]
    shards = {0: shard, 1: partner(shard, "tensor", 2)}
    for j in (2, 6, 4):
        shards[j] = partner(shard, "tensor", 2 * j)
    for j in (2, 6, 4):
        shards[j ^ 1] = partner(shards[1], "tensor", 2 * j)
    cot_other = partner(cot, "tensor", 2)
    own, cot_pair = stack("stack_tokens", order, [shards[j] for j in range(8)], [cot, cot_other])
    other = partner(own, "tensor", 1)
    cot_near = y_near([cot_pair] * 4)

    blocks = dict(zip((0, 1, 3), pick_tokens("pick_near", order, own, (0, 1, 3))))
    token_near = near(blocks)
    normed, inverse, own_tokens = norm(order, gain_row, own, other)
    rot, kv_own = project(order, normed, q_weight, kv_weight, tables)
    blocks[2], cot_copy = pick_tokens("pick_far", order, own, (2,), cot_pair)
    cot_far = y_far([cot_copy] * 4)
    kv_other = partner(kv_own, "tensor", 1)
    token_far = far(blocks)
    order.wait(*token_near.values(), *cot_near.values())
    attn, probs = attend(order, rot, kv_own, kv_other)
    send, keep = mix(order, attn, o_weight)
    arrived = partner(send, "tensor", 1)

    order.wait(*token_far.values())
    (cot_own,) = stack("stack_cot", order, in_order({0: cot_pair}, cot_near, cot_far))
    cot_other = partner(cot_own, "tensor", 1)

    def cot_plan(at_ref, ins, outs):
        return [
            (ins[0].at[at_ref[CHIP] ^ (2 * (at_ref[Z] ^ k) + x)], outs[k].at[x])
            for k in range(4)
            for x in range(2)
        ] + [(ins[1], outs[k].at[2]) for k in range(4)]

    cot_blocks = move(
        "pick_cot", order, [cot_own, attn], [shape((3, length, width))] * 4, cot_plan
    )
    b_near = near(cot_blocks)
    a_keep, a_send = split_x(
        "split_tokens", order, in_order({0: blocks[0]}, token_near, token_far)
    )
    a_cross = partner(a_send, "dp", 1)
    out_parts = pair_sum(order, keep, arrived, 4, Y)
    out_near = y_near(out_parts)
    dattn, own_cot = out_gradient(order, cot_own, cot_other, o_weight)
    dq, dkv_keep, send = attend_gradient(order, dattn, probs, rot, kv_own, kv_other, tables)
    arrived = partner(send, "tensor", 1)
    order.wait(*b_near.values(), *out_near.values(), a_cross)
    dqkv, scaled = join_gradient(order, dq, dkv_keep, arrived, inverse, tables)
    scaled_other = partner(scaled, "dp", 1)
    b_far = far(cot_blocks)
    out_far = y_far(out_parts)
    send, keep, gain_part = norm_gradient(order, dqkv, q_weight, kv_weight, normed, gain_row)
    arrived = partner(send, "tensor", 1)
    x_parts = pair_sum(order, keep, arrived, 4, Y)
    x_near = y_near(x_parts)
    gain_part = jnp.sum(lax.all_to_all(gain_part, "dp", 0, 0, tiled=True), axis=0)
    gain_part = lax.all_to_all(
        jnp.broadcast_to(gain_part[None], (16, 1, 2 * width)), "tensor", 0, 0, tiled=True
    )
    gain_grad = jnp.sum(gain_part, axis=0)
    order.wait(*b_far.values(), *out_far.values(), *x_near.values(), gain_grad)
    pair, a_own = stack("stack_dqkv", order, [scaled, scaled_other], [a_keep, a_cross])
    dqkv_near = near([pair] * 4)
    b_own, attn_all = stack_b(order, in_order({0: cot_blocks[0]}, b_near, b_far))
    b_other = partner(b_own, "tensor", 1)
    x_far = y_far(x_parts)
    (keep,) = out_terms("out_keep", order, b_own, b_other, attn_all, True)
    out_keep, out_send = ring_sum(order, in_order({0: out_parts[0]}, out_near, out_far))
    out_arrived = partner(out_send, "tensor", 2)
    x_keep, x_send = ring_sum(order, in_order({0: x_parts[0]}, x_near, x_far))
    x_arrived = partner(x_send, "tensor", 2)
    order.wait(*dqkv_near.values())
    send, pair_copy = out_terms("out_send", order, b_own, b_other, attn_all, False, pair)
    o_arrived = partner(send, "dp", 1)
    dqkv_far = far([pair_copy] * 4)
    a_other = partner(a_own, "tensor", 1)
    result = (own_tokens.astype(f32) + (out_keep + out_arrived.astype(f32))).astype(bf16)
    order.vmem = LATE
    q_grad, kv_grad = q_gradient(
        order,
        a_own,
        a_other,
        in_order({0: pair}, dqkv_near, dqkv_far),
        gain_column,
        q_width,
    )
    order.vmem = VMEM
    order.wait(o_arrived)
    x_grad = input_gradient(order, x_keep, x_arrived, own_tokens, inverse, own_cot, gain_row)
    o_grad = add_terms(order, keep, o_arrived)
    return (result[None], x_grad[None], gain_grad.reshape(-1), q_grad, kv_grad, o_grad)


def solution(mesh):
    in_specs = (
        P("dp", None, "tensor"),
        P(),
        P(None, "tensor"),
        P(None, "tensor"),
        P("tensor", None),
        P("dp", None, "tensor"),
    )
    out_specs = (
        P("dp", "tensor", None),
        P("dp", "tensor", None),
        P("dp"),
        P("dp", "tensor"),
        P("dp", "tensor"),
        P("tensor", "dp"),
    )
    return jax.shard_map(
        on_device, mesh=mesh, in_specs=in_specs, out_specs=out_specs, check_vma=False
    )
```
